32 devices in a mesh: grp: 2 (over x), tr: 8 (over z, y), ev: 2 (over core).
Axes of the slice: x: 2, y: 2, z: 4, core: 2. Of those that a mesh axis runs over, the one named last changes fastest.
Arguments:
- train_grads: bfloat16 [16384, 1024], P(('grp', 'tr', 'ev')), parts along dimension 0, may hold values from -80 to 80, as said below
- eval_grads: bfloat16 [8192, 1024], P(('grp', 'ev'), 'tr'), parts along dimension 0, may hold values from -6 to 6
- eval_bucket: int32 [8192], P(('grp', 'ev')), parts along dimension 0, may hold values from 0 to 7
- train_valid: int32 [16384], P(('grp', 'tr', 'ev')), parts along dimension 0, may hold values 0 or 1
Outputs:
- scores: bfloat16 [8192, 8192], P(('grp', 'ev'), 'tr'), parts along dimension 0
The draws below stay inside these ranges and needn't reach their ends.
There are 2 independent parts, one for each index of `grp`. The reference program is written for one: setup_inputs(seed, part) draws one part's arguments, and reference() takes and returns one part's arrays. A program takes and returns all parts, laid end to end along the dimension named above; each array names one. Nothing has to cross between parts.
Inputs may be any that keep to these rules, and one draw needn't show every extreme that they name: `train_grads`: real-valued projected gradients.
All inputs are finite; a program needn't handle non-finite values. No bound on the sum of `train_valid` on one device may be relied on, other than what follows from the above.
Results may differ from the reference program's by a relative error of at most 0.012.
Values may be sent and summed in bfloat16 or wider, within the bound.
No kernel may reach another device: no remote copies, remote signals or barrier semaphores. Data moves between devices by JAX's collectives and lax.ppermute only.
A program may use at most 128 MiB of HBM per device.

```python
import jax
import jax.numpy as jnp
from jax import lax

K = 1024
BUCKETS = 8
NTR = 8192
NEV = 4096


def draw_train_grads(key, part):
    key = jax.random.fold_in(key, 11)
    key_base, key_cols, key_rows = jax.random.split(key, 3)
    col_scale = jnp.exp(jax.random.uniform(key_cols, (1, K), jnp.float32, jnp.log(0.3), jnp.log(3.0)))
    position = jnp.arange(NTR, dtype=jnp.float32)[:, None] / NTR
    row_scale = (1.0 + 2.0 * position) * jnp.exp(jax.random.uniform(key_rows, (NTR, 1), jnp.float32, -0.35, 0.35))
    base = jnp.clip(jax.random.normal(key_base, (NTR, K), jnp.float32), -6.0, 6.0)
    values = base * col_scale * row_scale
    return values.astype(jnp.bfloat16)


def place_ends(values, key, smallest, high):
    dims = values.shape
    index_at = [jax.random.randint(jax.random.fold_in(key, axis), (), 0, dims[axis]) for axis in range(len(dims))]
    values = values.at[tuple(index_at)].set(smallest)
    longest = dims.index(max(dims))
    index_at[longest] = (index_at[longest] + 1) % dims[longest]
    return values.at[tuple(index_at)].set(high)


def shard_levels(own_key, extent, pieces, least, top_value):
    level, own = 1.0, jax.random.fold_in(own_key, 6)
    for dim, shards_of in pieces:
        draws = jnp.exp(jax.random.uniform(jax.random.fold_in(own, dim), (shards_of,), jnp.float32, least / len(pieces), top_value / len(pieces)))
        level = level * jnp.repeat(draws, extent[dim] // shards_of).reshape([-1 if axis == dim else 1 for axis in range(len(extent))])
    return level


def centred(rng, extent, width, most, cuts=(), held_as=jnp.bfloat16):
    gain = shard_levels(rng, extent, cuts, -0.22, 0.18) if cuts else 1.0
    entries = jax.random.normal(rng, extent, jnp.float32) * width * gain
    return jnp.minimum(jnp.maximum(entries, -most), most).astype(held_as)


def setup_inputs(seed: int = 0, part: int = 0) -> dict:
    streams_of = jax.random.split(jax.random.key(seed), 5)
    part_splits = jax.random.split(jax.random.fold_in(streams_of[4], part), 5)
    train_grads = draw_train_grads(jax.random.fold_in(jax.random.fold_in(streams_of[4], part), 71), part)
    eval_grads = centred(part_splits[1], (NEV, K), 1.0, 6.0, ((0, 2), (1, 8)))
    eval_bucket = place_ends(jax.random.randint(part_splits[2], (NEV,), 0, BUCKETS), jax.random.fold_in(part_splits[2], 1), 0, BUCKETS - 1).astype(jnp.int32)
    train_valid = place_ends((jax.random.randint(part_splits[3], (NTR,), 0, 4) < 3).astype(jnp.int32), jax.random.fold_in(part_splits[3], 1), 0, 1)
    return dict(train_grads=train_grads, eval_grads=eval_grads, eval_bucket=eval_bucket, train_valid=train_valid)


damping = 0.1
weight_table = (0.6, 0.9, 1.3, 1.8, 2.4, 3.1, 3.9, 4.8)

def chol_solve(factor, right):
    lower_solved = lax.linalg.triangular_solve(factor, right, left_side=True, lower=True)
    return lax.linalg.triangular_solve(factor, lower_solved, left_side=True, lower=True, transpose_a=True)

def reference(train_grads, eval_grads, eval_bucket, train_valid):
    masked = train_grads * train_valid[:, None].astype(jnp.bfloat16)
    gram = jnp.dot(masked.T.astype(jnp.float32), train_grads.astype(jnp.float32), preferred_element_type=jnp.float32)
    hessian = gram / NTR + damping * jnp.eye(K, dtype=jnp.float32)
    factor = jnp.linalg.cholesky(hessian)
    inverse = chol_solve(factor, jnp.eye(K, dtype=jnp.float32)).astype(jnp.bfloat16)
    precond = jnp.dot(masked.astype(jnp.float32), inverse.astype(jnp.float32), preferred_element_type=jnp.float32).astype(jnp.bfloat16)
    levels = jnp.arange(BUCKETS, dtype=jnp.int32)
    table_vals = jnp.array(weight_table, dtype=jnp.float32)
    weights = lax.optimization_barrier(jnp.sum(jnp.where(eval_bucket[:, None] == levels[None, :], table_vals[None, :], 0.0), axis=1)) / jnp.sqrt(jnp.float32(K))
    block_rows = min(NTR, 8192)
    blocks = precond.reshape(NTR // block_rows, block_rows, K)

    def one_block(piece):
        return (jnp.dot(eval_grads.astype(jnp.float32), piece.T.astype(jnp.float32), preferred_element_type=jnp.float32) * weights[:, None]).astype(jnp.bfloat16)
    result = lax.map(one_block, blocks)
    return jnp.transpose(result, (1, 0, 2)).reshape(NEV, NTR)
```

```python
import functools

import jax
import jax.numpy as jnp
from jax import lax
from jax.experimental import pallas as pl
from jax.experimental.pallas import tpu as pltpu
from jax.sharding import PartitionSpec as P

BUCKETS = 8
BLK = 128
MIB = 2**20

damping = 0.1
weight_table = (0.6, 0.9, 1.3, 1.8, 2.4, 3.1, 3.9, 4.8)

VMEM = pl.BlockSpec(memory_space=pltpu.VMEM)
SMEM = pl.BlockSpec(memory_space=pltpu.SMEM)


def split3(x):
    hi = x.astype(jnp.bfloat16)
    rest = x - hi.astype(jnp.float32)
    mid = rest.astype(jnp.bfloat16)
    low = (rest - mid.astype(jnp.float32)).astype(jnp.bfloat16)
    return hi, mid, low


def as_left(x):
    hi, mid, low = split3(x)
    return jnp.concatenate([hi, mid, hi, mid, hi, low], axis=1)


def as_right(x):
    hi, mid, low = split3(x)
    return jnp.concatenate([hi, hi, mid, mid, low, hi], axis=0)


def mm(left, right):
    return jnp.dot(left, right, preferred_element_type=jnp.float32)


def across(x, lane):
    return jnp.broadcast_to(x[:, lane : lane + 1], x.shape)


def down(x, row):
    return jnp.broadcast_to(x[row : row + 1, :], x.shape)


def invert_block(block):
    lanes = lax.broadcasted_iota(jnp.int32, (8, BLK), 1)
    subs = lax.broadcasted_iota(jnp.int32, (8, BLK), 0)
    strips = [block[8 * b : 8 * b + 8, :] for b in range(BLK // 8)]
    for m in range(BLK // 8):
        row = strips[m]
        cols = [across(row, 8 * m + t) for t in range(8)]
        for t in range(8):
            pivot = 1.0 / down(cols[t], t)
            here = subs == t
            own = lanes == 8 * m + t
            lead = jnp.where(own, 1.0, down(row, t)) * pivot
            row = jnp.where(here, lead, jnp.where(own, 0.0, row) - cols[t] * lead)
            for s in range(t + 1, 8):
                lead_s = down(cols[s], t)
                cols[s] = jnp.where(here, lead_s * pivot, cols[s] - (cols[t] * lead_s) * pivot)
        strips[m] = row
        done = (lanes >= 8 * m) & (lanes < 8 * m + 8)
        leads = [down(row, t) for t in range(8)]
        for b in range(BLK // 8):
            if b != m:
                old = strips[b]
                new = jnp.where(done, 0.0, old)
                for t in range(8):
                    new = new - across(old, 8 * m + t) * leads[t]
                strips[b] = new
    return jnp.concatenate(strips, axis=0)


def eliminate(src, dst):
    size = src.shape[0]
    rest = size - BLK
    pivot = invert_block(src[0:BLK, 0:BLK])
    right = src[0:BLK, BLK:size]
    left = src[BLK:size, 0:BLK]
    scaled = mm(as_left(pivot), as_right(right))
    left_parts = as_left(left)
    dst[0:rest, rest:size] = -mm(left_parts, as_right(pivot))
    dst[rest:size, 0:rest] = scaled
    dst[rest:size, rest:size] = pivot
    step = 256
    for at in range(0, rest, step):
        n = min(step, rest - at)
        dst[0:rest, at : at + n] = src[BLK:size, BLK + at : BLK + at + n] - mm(
            left_parts, as_right(scaled[:, at : at + n])
        )


def gram_kernel(masked_ref, gram_ref, turned_ref):
    turned_ref[...] = masked_ref[...].T
    blocks = masked_ref.shape[1] // BLK
    half = blocks // 2
    for i in range(half):
        part = mm(
            turned_ref[i * BLK : (i + 1) * BLK, :],
            masked_ref[:, i * BLK : (i + half + 1) * BLK],
        )
        for j in range(half + 1):
            at = (i * (half + 1) + j) * BLK
            gram_ref[at : at + BLK, :] = part[:, j * BLK : (j + 1) * BLK]


def inverse_kernel(total_rows, ev_ref, own_ref, other_ref, out_ref, one, two):
    size = out_ref.shape[0]
    blocks = size // BLK
    half = blocks // 2
    rows = lax.broadcasted_iota(jnp.int32, (BLK, BLK), 0)
    cols = lax.broadcasted_iota(jnp.int32, (BLK, BLK), 1)
    ridge = jnp.where(rows == cols, jnp.float32(damping), 0.0)
    for i in range(blocks):
        source = own_ref if i < half else other_ref
        for j in range(half + 1):
            at = ((i % half) * (half + 1) + j) * BLK
            c = (i + j) % blocks
            value = source[at : at + BLK, :] / total_rows
            if j == 0:
                value = value + ridge
            one[i * BLK : (i + 1) * BLK, c * BLK : (c + 1) * BLK] = value
            if 0 < j < half:
                one[c * BLK : (c + 1) * BLK, i * BLK : (i + 1) * BLK] = value.T

    @pl.loop(0, blocks // 2)
    def _(_):
        eliminate(one, two)
        eliminate(two, one)

    here = ev_ref[0]
    for i in range(blocks):
        to = lax.rem(i + half * here, blocks) * BLK
        out_ref[pl.ds(pl.multiple_of(to, BLK), BLK), :] = one[i * BLK : (i + 1) * BLK, :].astype(jnp.bfloat16)


def score_kernel(eval_ref, weight_ref, inverse_ref, turned_ref, out_ref, precond):
    @pl.when(pl.program_id(0) == 0)
    def _():
        precond[...] = mm(inverse_ref[...], turned_ref[...]).astype(jnp.bfloat16)

    out_ref[...] = (mm(eval_ref[...], precond[...]) * weight_ref[...]).astype(jnp.bfloat16)


def shards(train_grads, eval_grads, eval_bucket, train_valid):
    rows_here, width = train_grads.shape
    total_rows = rows_here * lax.axis_size("tr") * lax.axis_size("ev")
    here = lax.axis_index("ev")
    swap = [(0, 1), (1, 0)]

    masked = train_grads * train_valid[:, None].astype(jnp.bfloat16)
    other_masked = lax.ppermute(masked, "ev", swap)
    chip = jnp.where(
        here == 0,
        jnp.concatenate([masked, other_masked], axis=0),
        jnp.concatenate(
            [jnp.roll(other_masked, width // 2, axis=1), jnp.roll(masked, width // 2, axis=1)], axis=0
        ),
    )
    chip_rows = 2 * rows_here
    held = (width // BLK // 2) * (width // BLK // 2 + 1) * BLK
    local_gram, turned = pl.pallas_call(
        gram_kernel,
        out_shape=(
            jax.ShapeDtypeStruct((held, BLK), jnp.float32),
            jax.ShapeDtypeStruct((width, chip_rows), jnp.bfloat16),
        ),
        in_specs=[VMEM],
        out_specs=(VMEM, VMEM),
        compiler_params=pltpu.CompilerParams(vmem_limit_bytes=32 * MIB),
        cost_estimate=pl.CostEstimate(flops=2 * chip_rows * held * BLK, bytes_accessed=6 * MIB, transcendentals=0),
        name="gram",
    )(chip)
    own_gram = lax.psum(local_gram, "tr")
    other_gram = lax.ppermute(own_gram, "ev", swap)
    eval_grads, own_gram = lax.optimization_barrier((eval_grads, own_gram))
    full_eval = lax.all_gather(eval_grads, "tr", axis=1, tiled=True)

    inverse = pl.pallas_call(
        functools.partial(inverse_kernel, total_rows),
        out_shape=jax.ShapeDtypeStruct((width, width), jnp.bfloat16),
        in_specs=[SMEM, VMEM, VMEM],
        out_specs=VMEM,
        scratch_shapes=[pltpu.VMEM((width, width), jnp.float32)] * 2,
        compiler_params=pltpu.CompilerParams(vmem_limit_bytes=48 * MIB),
        cost_estimate=pl.CostEstimate(flops=40_000_000_000, bytes_accessed=5 * MIB, transcendentals=0),
        name="inverse",
    )(here.reshape(1), own_gram, other_gram)

    levels = jnp.arange(BUCKETS, dtype=jnp.int32)
    table_vals = jnp.array(weight_table, dtype=jnp.float32)
    weights = jnp.sum(
        jnp.where(eval_bucket[:, None] == levels[None, :], table_vals[None, :], 0.0), axis=1
    ) / jnp.sqrt(jnp.float32(width))
    eval_rows = full_eval.shape[0]
    tile = 256
    return pl.pallas_call(
        score_kernel,
        grid=(eval_rows // tile,),
        out_shape=jax.ShapeDtypeStruct((eval_rows, chip_rows), jnp.bfloat16),
        in_specs=[
            pl.BlockSpec((tile, width), lambda i: (i, 0)),
            pl.BlockSpec((tile, 1), lambda i: (i, 0)),
            pl.BlockSpec((width, width), lambda i: (0, 0)),
            pl.BlockSpec((width, chip_rows), lambda i: (0, 0)),
        ],
        out_specs=pl.BlockSpec((tile, chip_rows), lambda i: (i, 0)),
        scratch_shapes=[pltpu.VMEM((width, chip_rows), jnp.bfloat16)],
        compiler_params=pltpu.CompilerParams(vmem_limit_bytes=40 * MIB),
        cost_estimate=pl.CostEstimate(
            flops=2 * (eval_rows + width) * width * chip_rows, bytes_accessed=12 * MIB, transcendentals=0
        ),
        name="scores",
    )(full_eval, weights[:, None], inverse, turned)


def solution(mesh):
    in_specs = (
        P(("grp", "tr", "ev"), None),
        P(("grp", "ev"), "tr"),
        P(("grp", "ev")),
        P(("grp", "tr", "ev")),
    )
    out_specs = P(("grp", "ev"), "tr")
    return jax.shard_map(shards, mesh=mesh, in_specs=in_specs, out_specs=out_specs, check_vma=False)
```

```python
import functools

import jax
import jax.numpy as jnp
from jax import lax
from jax.experimental import pallas as pl
from jax.experimental.pallas import tpu as pltpu
from jax.sharding import PartitionSpec as P

BUCKETS = 8
BLK = 128
MIB = 2**20

damping = 0.1
weight_table = (0.6, 0.9, 1.3, 1.8, 2.4, 3.1, 3.9, 4.8)

VMEM = pl.BlockSpec(memory_space=pltpu.VMEM)
SMEM = pl.BlockSpec(memory_space=pltpu.SMEM)

def split3(x):
    hi = x.astype(jnp.bfloat16)
    rest = x - hi.astype(jnp.float32)
    mid = rest.astype(jnp.bfloat16)
    low = (rest - mid.astype(jnp.float32)).astype(jnp.bfloat16)
    return hi, mid, low


def as_left(x):
    hi, mid, low = split3(x)
    return jnp.concatenate([hi, mid, hi, mid, hi, low], axis=1)


def as_right(x):
    hi, mid, low = split3(x)
    return jnp.concatenate([hi, hi, mid, mid, low, hi], axis=0)


def mm(left, right):
    return jnp.dot(left, right, preferred_element_type=jnp.float32)


def across(x, lane):
    return jnp.broadcast_to(x[:, lane : lane + 1], x.shape)


def down(x, row):
    return jnp.broadcast_to(x[row : row + 1, :], x.shape)


def total(terms):
    while len(terms) > 1:
        terms = [a + b for a, b in zip(terms[::2], terms[1::2])] + terms[len(terms) & ~1 :]
    return terms[0]


def invert_block(block, beside=()):
    lanes = lax.broadcasted_iota(jnp.int32, (8, BLK), 1)
    subs = lax.broadcasted_iota(jnp.int32, (8, BLK), 0)
    count = BLK // 8
    strips = [block[8 * b : 8 * b + 8, :] for b in range(count)]
    for m in range(count):
        row = strips[m]
        cols = [across(row, 8 * m + t) for t in range(8)]
        for t in range(0, 8, 2):
            first, second = cols[t], cols[t + 1]
            a, b, c = down(first, t), down(second, t), down(second, t + 1)
            scale = 1.0 / (a * c - b * b)
            at_first, at_second = subs == t, subs == t + 1
            own_first, own_second = lanes == 8 * m + t, lanes == 8 * m + t + 1
            upper = jnp.where(own_first, 1.0, jnp.where(own_second, 0.0, down(row, t)))
            lower = jnp.where(own_second, 1.0, jnp.where(own_first, 0.0, down(row, t + 1)))
            lead_first = c * upper - b * lower
            lead_second = a * lower - b * upper
            swept = first * lead_first + second * lead_second
            rest = jnp.where(own_first | own_second, 0.0, row) - swept * scale
            row = jnp.where(at_first, lead_first * scale, jnp.where(at_second, lead_second * scale, rest))
            for s in range(t + 2, 8):
                upper, lower = down(cols[s], t), down(cols[s], t + 1)
                lead_first = c * upper - b * lower
                lead_second = a * lower - b * upper
                swept = first * lead_first + second * lead_second
                cols[s] = jnp.where(
                    at_first,
                    lead_first * scale,
                    jnp.where(at_second, lead_second * scale, cols[s] - swept * scale),
                )
        strips[m] = row
        done = (lanes >= 8 * m) & (lanes < 8 * m + 8)
        leads = [down(row, t) for t in range(8)]
        for b in [*range(m + 1, count), *range(m)]:
            old = strips[b]
            strips[b] = jnp.where(done, 0.0, old) - total([across(old, 8 * m + t) * leads[t] for t in range(8)])
        if m < len(beside):
            beside[m]()
    return jnp.concatenate(strips, axis=0)


def eliminate(src, dst, held, left_ref, right_ref, last=False):
    size = src.shape[0]
    rest = size - BLK
    pivot = held[...]
    scaled = mm(as_left(pivot), as_right(src[0:BLK, BLK:size]))
    left_ref[...] = as_left(src[BLK:size, 0:BLK])
    right_ref[...] = as_right(scaled)
    dst[rest:size, 0:rest] = scaled
    dst[rest:size, rest:size] = pivot

    def strip(top, tall, at, wide):
        def run():
            dst[top : top + tall, at : at + wide] = src[
                BLK + top : BLK + top + tall, BLK + at : BLK + at + wide
            ] - mm(left_ref[top : top + tall, :], right_ref[:, at : at + wide])

        return run

    def border():
        dst[0:rest, rest:size] = -mm(left_ref[...], as_right(pivot))

    wide = 2 * BLK
    work = [strip(0, rest, at, min(wide, rest - at)) for at in range(0, rest, wide)] + [border]
    if last:
        for piece in work:
            piece()
    else:
        ahead = src[BLK : 2 * BLK, BLK : 2 * BLK] - mm(left_ref[0:BLK, :], right_ref[:, 0:BLK])
        spread = []
        for piece in work:
            spread += [piece, lambda: None]
        held[...] = invert_block(ahead, spread)


def gram_kernel(ev_ref, own_ref, other_ref, valid_ref, *refs):
    parts, turned_ref, chip = refs[:-2], refs[-2], refs[-1]
    here = ev_ref[0]
    rows, width = own_ref.shape
    blocks = width // BLK
    half = blocks // 2
    middle = width // 2
    for order, ref in ((here, own_ref), (1 - here, other_ref)):
        at = pl.ds(pl.multiple_of(order * rows, rows), rows)
        for side in range(2):
            to = pl.ds(pl.multiple_of((here + side) % 2 * middle, middle), middle)
            piece = ref[:, side * middle : (side + 1) * middle]
            chip[at, to] = piece
            turned_ref[to, at] = piece.T
    turned_ref[...] = turned_ref[...] * valid_ref[...].astype(jnp.float32).astype(jnp.bfloat16)
    each = half * (half + 1) // len(parts)
    for i in range(half):
        part = mm(
            turned_ref[i * BLK : (i + 1) * BLK, :],
            chip[:, i * BLK : (i + half + 1) * BLK],
        )
        for j in range(half + 1):
            n = i * (half + 1) + j
            at = n % each * BLK
            parts[n // each][at : at + BLK, :] = part[:, j * BLK : (j + 1) * BLK]


def inverse_kernel(total_rows, ev_ref, *refs):
    *parts, out_ref, one, two, held, left_ref, right_ref = refs
    size = out_ref.shape[0]
    blocks = size // BLK
    half = blocks // 2
    each = parts[0].shape[0] // BLK
    rows = lax.broadcasted_iota(jnp.int32, (BLK, BLK), 0)
    cols = lax.broadcasted_iota(jnp.int32, (BLK, BLK), 1)
    ridge = jnp.where(rows == cols, jnp.float32(damping), 0.0)
    for i in range(blocks):
        for j in range(half + 1):
            n = i * (half + 1) + j
            at = n % each * BLK
            c = (i + j) % blocks
            value = parts[n // each][at : at + BLK, :] / total_rows
            if j == 0:
                value = value + ridge
            one[i * BLK : (i + 1) * BLK, c * BLK : (c + 1) * BLK] = value
            if 0 < j < half:
                one[c * BLK : (c + 1) * BLK, i * BLK : (i + 1) * BLK] = value.T

    held[...] = invert_block(one[0:BLK, 0:BLK])

    @pl.loop(0, blocks // 2 - 1)
    def _(_):
        eliminate(one, two, held, left_ref, right_ref)
        eliminate(two, one, held, left_ref, right_ref)

    eliminate(one, two, held, left_ref, right_ref)
    eliminate(two, one, held, left_ref, right_ref, last=True)
    here = ev_ref[0]
    for i in range(blocks):
        to = lax.rem(i + half * here, blocks) * BLK
        out_ref[pl.ds(pl.multiple_of(to, BLK), BLK), :] = one[i * BLK : (i + 1) * BLK, :].astype(jnp.bfloat16)


def score_kernel(eval_ref, weight_ref, inverse_ref, turned_ref, out_ref, precond):
    @pl.when(pl.program_id(0) == 0)
    def _():
        precond[...] = mm(inverse_ref[...], turned_ref[...]).astype(jnp.bfloat16)

    out_ref[...] = (mm(eval_ref[...], precond[...]) * weight_ref[...]).astype(jnp.bfloat16)


def shift(members, stride, by):
    n = lax.axis_size("tr")
    pairs = []
    for i in range(n):
        p = i // stride % members
        pairs.append((i, i + ((p + by) % members - p) * stride))
    return pairs


def scatter_sum(x, members, stride):
    me = lax.axis_index("tr") // stride % members
    chunks = x.reshape(members, -1, BLK)
    mine = lax.dynamic_index_in_dim(chunks, me, keepdims=False)
    got = [
        lax.ppermute(
            lax.dynamic_index_in_dim(chunks, (me + by) % members, keepdims=False), "tr", shift(members, stride, by)
        )
        for by in range(1, members)
    ]
    for piece in got:
        mine = mine + piece
    return mine


def collect(x, members, stride):
    me = lax.axis_index("tr") // stride % members
    got = [x] + [lax.ppermute(x, "tr", shift(members, stride, by)) for by in range(members - 1, 0, -1)]
    if members == 2:
        whole = jnp.where(
            me == 0, jnp.concatenate(got, axis=0), jnp.concatenate(got[::-1], axis=0)
        )
        return whole
    twice = jnp.concatenate(got + got, axis=0)
    return lax.dynamic_slice_in_dim(twice, (members - me) * x.shape[0], members * x.shape[0])


def sum_over_tr(parts):
    n = lax.axis_size("tr")
    inner = 2 ** ((n.bit_length() - 1) // 2)
    axes = [(inner, 1), (n // inner, inner)]
    orders = [axes, axes[::-1]]
    parts = [scatter_sum(x, *order[0]) for x, order in zip(parts, orders)]
    parts = [scatter_sum(x, *order[1]) for x, order in zip(parts, orders)]
    parts = [collect(x, *order[1]) for x, order in zip(parts, orders)]
    return [collect(x, *order[0]) for x, order in zip(parts, orders)]


def shards(train_grads, eval_grads, eval_bucket, train_valid):
    rows_here, width = train_grads.shape
    total_rows = rows_here * lax.axis_size("tr") * lax.axis_size("ev")
    here = lax.axis_index("ev")
    swap = [(0, 1), (1, 0)]
    full_eval = lax.all_gather(eval_grads, "tr", axis=1, tiled=True)

    other_train = lax.ppermute(train_grads, "ev", swap)
    other_valid = lax.ppermute(train_valid, "ev", swap)
    chip_valid = jnp.where(
        here == 0, jnp.concatenate([train_valid, other_valid]), jnp.concatenate([other_valid, train_valid])
    )
    chip_rows = 2 * rows_here
    half = width // BLK // 2
    held = half * (half + 1) * BLK
    *local_gram, turned = pl.pallas_call(
        gram_kernel,
        out_shape=(
            *[jax.ShapeDtypeStruct((held // 2, BLK), jnp.float32)] * 2,
            jax.ShapeDtypeStruct((width, chip_rows), jnp.bfloat16),
        ),
        in_specs=[SMEM, VMEM, VMEM, VMEM],
        out_specs=(VMEM,) * 3,
        scratch_shapes=[pltpu.VMEM((chip_rows, width), jnp.bfloat16)],
        compiler_params=pltpu.CompilerParams(vmem_limit_bytes=56 * MIB),
        cost_estimate=pl.CostEstimate(flops=2 * chip_rows * held * BLK, bytes_accessed=6 * MIB, transcendentals=0),
        name="gram",
    )(here.reshape(1), train_grads, other_train, chip_valid[None, :])
    own_gram = sum_over_tr(local_gram)
    other_gram = [lax.ppermute(x, "ev", swap) for x in own_gram]

    inverse = pl.pallas_call(
        functools.partial(inverse_kernel, total_rows),
        out_shape=jax.ShapeDtypeStruct((width, width), jnp.bfloat16),
        in_specs=[SMEM] + [VMEM] * 4,
        out_specs=VMEM,
        scratch_shapes=[
            pltpu.VMEM((width, width), jnp.float32),
            pltpu.VMEM((width, width), jnp.float32),
            pltpu.VMEM((BLK, BLK), jnp.float32),
            pltpu.VMEM((width - BLK, 6 * BLK), jnp.bfloat16),
            pltpu.VMEM((6 * BLK, width - BLK), jnp.bfloat16),
        ],
        compiler_params=pltpu.CompilerParams(vmem_limit_bytes=56 * MIB),
        cost_estimate=pl.CostEstimate(flops=30_000_000_000, bytes_accessed=5 * MIB, transcendentals=0),
        name="inverse",
    )(here.reshape(1), *own_gram, *other_gram)

    levels = jnp.arange(BUCKETS, dtype=jnp.int32)
    table_vals = jnp.array(weight_table, dtype=jnp.float32)
    weights = jnp.sum(
        jnp.where(eval_bucket[:, None] == levels[None, :], table_vals[None, :], 0.0), axis=1
    ) / jnp.sqrt(jnp.float32(width))
    eval_rows = full_eval.shape[0]
    tile = 256
    return pl.pallas_call(
        score_kernel,
        grid=(eval_rows // tile,),
        out_shape=jax.ShapeDtypeStruct((eval_rows, chip_rows), jnp.bfloat16),
        in_specs=[
            pl.BlockSpec((tile, width), lambda i: (i, 0)),
            pl.BlockSpec((tile, 1), lambda i: (i, 0)),
            pl.BlockSpec((width, width), lambda i: (0, 0)),
            pl.BlockSpec((width, chip_rows), lambda i: (0, 0)),
        ],
        out_specs=pl.BlockSpec((tile, chip_rows), lambda i: (i, 0)),
        scratch_shapes=[pltpu.VMEM((width, chip_rows), jnp.bfloat16)],
        compiler_params=pltpu.CompilerParams(vmem_limit_bytes=56 * MIB),
        cost_estimate=pl.CostEstimate(
            flops=2 * (eval_rows + width) * width * chip_rows, bytes_accessed=12 * MIB, transcendentals=0
        ),
        name="scores",
    )(full_eval, weights[:, None], inverse, turned)


def solution(mesh):
    in_specs = (
        P(("grp", "tr", "ev"), None),
        P(("grp", "ev"), "tr"),
        P(("grp", "ev")),
        P(("grp", "tr", "ev")),
    )
    out_specs = P(("grp", "ev"), "tr")
    return jax.shard_map(shards, mesh=mesh, in_specs=in_specs, out_specs=out_specs, check_vma=False)
```

```python
import functools

import jax
import jax.numpy as jnp
from jax import lax
from jax.experimental import pallas as pl
from jax.experimental.pallas import tpu as pltpu
from jax.sharding import PartitionSpec as P

BUCKETS = 8
BLK = 128
MIB = 2**20

damping = 0.1
weight_table = (0.6, 0.9, 1.3, 1.8, 2.4, 3.1, 3.9, 4.8)

VMEM = pl.BlockSpec(memory_space=pltpu.VMEM)
SMEM = pl.BlockSpec(memory_space=pltpu.SMEM)

def split3(x):
    hi = x.astype(jnp.bfloat16)
    rest = x - hi.astype(jnp.float32)
    mid = rest.astype(jnp.bfloat16)
    low = (rest - mid.astype(jnp.float32)).astype(jnp.bfloat16)
    return hi, mid, low


def as_left(x):
    hi, mid, low = split3(x)
    return jnp.concatenate([hi, mid, hi, mid, hi, low], axis=1)


def as_right(x):
    hi, mid, low = split3(x)
    return jnp.concatenate([hi, hi, mid, mid, low, hi], axis=0)


def mm(left, right):
    return jnp.dot(left, right, preferred_element_type=jnp.float32)


def across(x, lane):
    return jnp.broadcast_to(x[:, lane : lane + 1], x.shape)


def down(x, row):
    return jnp.broadcast_to(x[row : row + 1, :], x.shape)


def total(terms):
    while len(terms) > 1:
        terms = [a + b for a, b in zip(terms[::2], terms[1::2])] + terms[len(terms) & ~1 :]
    return terms[0]


def invert_block(block, beside=()):
    lanes = lax.broadcasted_iota(jnp.int32, (8, BLK), 1)
    subs = lax.broadcasted_iota(jnp.int32, (8, BLK), 0)
    count = BLK // 8
    strips = [block[8 * b : 8 * b + 8, :] for b in range(count)]
    for m in range(count):
        row = strips[m]
        cols = [across(row, 8 * m + t) for t in range(8)]
        for t in range(0, 8, 2):
            first, second = cols[t], cols[t + 1]
            a, b, c = down(first, t), down(second, t), down(second, t + 1)
            scale = 1.0 / (a * c - b * b)
            at_first, at_second = subs == t, subs == t + 1
            own_first, own_second = lanes == 8 * m + t, lanes == 8 * m + t + 1
            upper = jnp.where(own_first, 1.0, jnp.where(own_second, 0.0, down(row, t)))
            lower = jnp.where(own_second, 1.0, jnp.where(own_first, 0.0, down(row, t + 1)))
            lead_first = c * upper - b * lower
            lead_second = a * lower - b * upper
            swept = first * lead_first + second * lead_second
            rest = jnp.where(own_first | own_second, 0.0, row) - swept * scale
            row = jnp.where(at_first, lead_first * scale, jnp.where(at_second, lead_second * scale, rest))
            for s in range(t + 2, 8):
                upper, lower = down(cols[s], t), down(cols[s], t + 1)
                lead_first = c * upper - b * lower
                lead_second = a * lower - b * upper
                swept = first * lead_first + second * lead_second
                cols[s] = jnp.where(
                    at_first,
                    lead_first * scale,
                    jnp.where(at_second, lead_second * scale, cols[s] - swept * scale),
                )
        strips[m] = row
        done = (lanes >= 8 * m) & (lanes < 8 * m + 8)
        leads = [down(row, t) for t in range(8)]
        for b in [*range(m + 1, count), *range(m)]:
            old = strips[b]
            strips[b] = jnp.where(done, 0.0, old) - total([across(old, 8 * m + t) * leads[t] for t in range(8)])
        if m < len(beside):
            beside[m]()
    return jnp.concatenate(strips, axis=0)


def eliminate(src, dst, held, left_ref, right_ref, last=False):
    size = src.shape[0]
    rest = size - BLK
    pivot = held[...]
    scaled = mm(as_left(pivot), as_right(src[0:BLK, BLK:size]))
    left_ref[...] = as_left(src[BLK:size, 0:BLK])
    right_ref[...] = as_right(scaled)
    dst[rest:size, 0:rest] = scaled
    dst[rest:size, rest:size] = pivot

    def strip(top, tall, at, wide):
        def run():
            dst[top : top + tall, at : at + wide] = src[
                BLK + top : BLK + top + tall, BLK + at : BLK + at + wide
            ] - mm(left_ref[top : top + tall, :], right_ref[:, at : at + wide])

        return run

    def border():
        dst[0:rest, rest:size] = -mm(left_ref[...], as_right(pivot))

    wide = 2 * BLK
    work = [strip(0, rest, at, min(wide, rest - at)) for at in range(0, rest, wide)] + [border]
    if last:
        for piece in work:
            piece()
    else:
        ahead = src[BLK : 2 * BLK, BLK : 2 * BLK] - mm(left_ref[0:BLK, :], right_ref[:, 0:BLK])
        spread = []
        for piece in work:
            spread += [piece, lambda: None]
        held[...] = invert_block(ahead, spread)


def gram_kernel(ev_ref, own_ref, other_ref, valid_ref, *refs):
    parts, turned_ref, chip = refs[:-2], refs[-2], refs[-1]
    here = ev_ref[0]
    rows, width = own_ref.shape
    blocks = width // BLK
    half = blocks // 2
    middle = width // 2
    for order, ref in ((here, own_ref), (1 - here, other_ref)):
        at = pl.ds(pl.multiple_of(order * rows, rows), rows)
        for side in range(2):
            to = pl.ds(pl.multiple_of((here + side) % 2 * middle, middle), middle)
            piece = ref[:, side * middle : (side + 1) * middle]
            chip[at, to] = piece
            turned_ref[to, at] = piece.T
    turned_ref[...] = turned_ref[...] * valid_ref[...].astype(jnp.float32).astype(jnp.bfloat16)
    each = half * (half + 1) // len(parts)
    for i in range(half):
        part = mm(
            turned_ref[i * BLK : (i + 1) * BLK, :],
            chip[:, i * BLK : (i + half + 1) * BLK],
        )
        for j in range(half + 1):
            n = i * (half + 1) + j
            at = n % each * BLK
            parts[n // each][at : at + BLK, :] = part[:, j * BLK : (j + 1) * BLK]


def inverse_kernel(total_rows, stages, first, last, *refs):
    if first:
        *parts, matrix_out, held_out, one, two, left_ref, right_ref = refs
    elif last:
        place_ref, matrix_in, held_in, turned_ref, out_ref, one, two, held_out, left_ref, right_ref = refs
    else:
        matrix_in, held_in, matrix_out, held_out, one, two, left_ref, right_ref = refs
    size = one.shape[0]
    blocks = size // BLK
    half = blocks // 2
    if first:
        each = parts[0].shape[0] // BLK
        rows = lax.broadcasted_iota(jnp.int32, (BLK, BLK), 0)
        cols = lax.broadcasted_iota(jnp.int32, (BLK, BLK), 1)
        ridge = jnp.where(rows == cols, jnp.float32(damping), 0.0)
        for i in range(blocks):
            for j in range(half + 1):
                n = i * (half + 1) + j
                at = n % each * BLK
                c = (i + j) % blocks
                value = parts[n // each][at : at + BLK, :] / total_rows
                if j == 0:
                    value = value + ridge
                one[i * BLK : (i + 1) * BLK, c * BLK : (c + 1) * BLK] = value
                if 0 < j < half:
                    one[c * BLK : (c + 1) * BLK, i * BLK : (i + 1) * BLK] = value.T
        held_out[...] = invert_block(one[0:BLK, 0:BLK])
        now = one
    else:
        held_out[...] = held_in[...]
        now = matrix_in
    for stage in range(stages):
        if stage == stages - 1 and not last:
            then = matrix_out
        else:
            then = one if now is two else two
        eliminate(now, then, held_out, left_ref, right_ref, last=last and stage == stages - 1)
        now = then
    if last:
        for i in range(blocks):
            part = mm(now[i * BLK : (i + 1) * BLK, :].astype(jnp.bfloat16), turned_ref[...])
            to = pl.multiple_of(place_ref[i] * BLK, BLK)
            out_ref[pl.ds(to, BLK), :] = part.astype(jnp.bfloat16)


def call_inverse(width, total_rows, stages, operands, first=False, last=False):
    state = (
        jax.ShapeDtypeStruct((width, width), jnp.float32),
        jax.ShapeDtypeStruct((BLK, BLK), jnp.float32),
    )
    result = jax.ShapeDtypeStruct((width, operands[-1].shape[-1]), jnp.bfloat16)
    return pl.pallas_call(
        functools.partial(inverse_kernel, total_rows, stages, first, last),
        out_shape=result if last else state,
        in_specs=[SMEM if x.ndim == 1 else VMEM for x in operands],
        out_specs=VMEM if last else (VMEM, VMEM),
        scratch_shapes=[
            pltpu.VMEM((width, width), jnp.float32),
            pltpu.VMEM((width, width), jnp.float32),
            *([pltpu.VMEM((BLK, BLK), jnp.float32)] if last else []),
            pltpu.VMEM((width - BLK, 6 * BLK), jnp.bfloat16),
            pltpu.VMEM((6 * BLK, width - BLK), jnp.bfloat16),
        ],
        compiler_params=pltpu.CompilerParams(vmem_limit_bytes=36 * MIB),
        cost_estimate=pl.CostEstimate(flops=stages * 6_000_000_000, bytes_accessed=4 * MIB, transcendentals=0),
        name="inverse",
    )(*operands)


def score_kernel(bucket_ref, precond_ref, *refs):
    *eval_refs, out_ref = refs
    width = precond_ref.shape[0]
    bucket = bucket_ref[0]
    weight = jnp.zeros(bucket.shape, jnp.float32)
    for level in range(BUCKETS):
        weight = weight + jnp.where(bucket == level, jnp.float32(weight_table[level]), 0.0)
    weight = weight / jnp.sqrt(jnp.float32(width))
    rows = out_ref.shape[0]
    evals = jnp.concatenate([ref[...] for ref in eval_refs], axis=1)
    scores = mm(evals, precond_ref[...])
    for at in range(0, rows, BLK):
        factor = jnp.broadcast_to(weight[:, at : at + BLK], (BLK, BLK)).T
        for to in range(0, out_ref.shape[1], BLK):
            out_ref[at : at + BLK, to : to + BLK] = (
                scores[at : at + BLK, to : to + BLK] * factor
            ).astype(jnp.bfloat16)


def shift(members, stride, by):
    n = lax.axis_size("tr")
    pairs = []
    for i in range(n):
        p = i // stride % members
        pairs.append((i, i + ((p + by) % members - p) * stride))
    return pairs


def scatter_sum(x, members, stride):
    me = lax.axis_index("tr") // stride % members
    chunks = x.reshape(members, -1, BLK)
    mine = lax.dynamic_index_in_dim(chunks, me, keepdims=False)
    got = [
        lax.ppermute(
            lax.dynamic_index_in_dim(chunks, (me + by) % members, keepdims=False), "tr", shift(members, stride, by)
        )
        for by in range(1, members)
    ]
    for piece in got:
        mine = mine + piece
    return mine


def collect(x, members, stride):
    me = lax.axis_index("tr") // stride % members
    got = [x] + [lax.ppermute(x, "tr", shift(members, stride, by)) for by in range(members - 1, 0, -1)]
    if members == 2:
        whole = jnp.where(
            me == 0, jnp.concatenate(got, axis=0), jnp.concatenate(got[::-1], axis=0)
        )
        return whole
    twice = jnp.concatenate(got + got, axis=0)
    return lax.dynamic_slice_in_dim(twice, (members - me) * x.shape[0], members * x.shape[0])


def chip_axes():
    n = lax.axis_size("tr")
    inner = 2 ** ((n.bit_length() - 1) // 2)
    return (inner, 1), (n // inner, inner)


def sum_over_tr(parts):
    axes = chip_axes()
    orders = [axes, axes[::-1]]
    parts = [scatter_sum(x, *order[0]) for x, order in zip(parts, orders)]
    parts = [scatter_sum(x, *order[1]) for x, order in zip(parts, orders)]
    parts = [collect(x, *order[1]) for x, order in zip(parts, orders)]
    return [collect(x, *order[0]) for x, order in zip(parts, orders)]


def shards(train_grads, eval_grads, eval_bucket, train_valid):
    rows_here, width = train_grads.shape
    total_rows = rows_here * lax.axis_size("tr") * lax.axis_size("ev")
    here = lax.axis_index("ev")
    tr = lax.axis_index("tr")
    swap = [(0, 1), (1, 0)]
    blocks = width // BLK
    half = blocks // 2
    (inner, _), (outer, _) = chip_axes()
    by_ring = eval_grads.shape[1] % BLK == 0

    def across_inner(x):
        return [lax.ppermute(x, "tr", shift(inner, 1, by)) for by in range(1, inner)]

    def along_outer(x):
        return lax.ppermute(x, "tr", shift(outer, inner, 1))

    other_train = lax.ppermute(train_grads, "ev", swap)
    other_valid = lax.ppermute(train_valid, "ev", swap)
    chip_valid = jnp.where(
        here == 0, jnp.concatenate([train_valid, other_valid]), jnp.concatenate([other_valid, train_valid])
    )
    chip_rows = 2 * rows_here
    held = half * (half + 1) * BLK
    *local_gram, turned = pl.pallas_call(
        gram_kernel,
        out_shape=(
            *[jax.ShapeDtypeStruct((held // 2, BLK), jnp.float32)] * 2,
            jax.ShapeDtypeStruct((width, chip_rows), jnp.bfloat16),
        ),
        in_specs=[SMEM, VMEM, VMEM, VMEM],
        out_specs=(VMEM,) * 3,
        scratch_shapes=[pltpu.VMEM((chip_rows, width), jnp.bfloat16)],
        compiler_params=pltpu.CompilerParams(vmem_limit_bytes=32 * MIB),
        cost_estimate=pl.CostEstimate(flops=2 * chip_rows * held * BLK, bytes_accessed=6 * MIB, transcendentals=0),
        name="gram",
    )(here.reshape(1), train_grads, other_train, chip_valid[None, :])

    ring = [eval_grads]
    beside = []
    if by_ring:
        ring.append(along_outer(eval_grads))
        beside.append(across_inner(eval_grads))

    own_gram = sum_over_tr(local_gram)
    other_gram = [lax.ppermute(x, "ev", swap) for x in own_gram]
    gram = [*own_gram, *other_gram]

    column = (jnp.arange(blocks, dtype=jnp.int32) + half * here) % blocks
    if by_ring:
        gram, ring, beside = lax.optimization_barrier((gram, ring, beside))
        owner = column * BLK // eval_grads.shape[1]
        behind = (tr // inner - owner // inner) % outer
        aside = (tr - owner) % inner
        each = eval_grads.shape[1] // BLK
        place = (behind * inner + aside) * each + column % each
    else:
        gram, eval_grads = lax.optimization_barrier((gram, eval_grads))
        full_eval = lax.all_gather(eval_grads, "tr", axis=1, tiled=True)
        place = column

    def advance():
        if by_ring and len(ring) < outer:
            arrived = ring[-1]
            ring.append(along_outer(arrived))
            beside.append(across_inner(arrived))

    advance()
    state = call_inverse(width, total_rows, 2, gram, first=True)
    if by_ring:
        state, ring, beside = lax.optimization_barrier((state, ring, beside))
    advance()
    state = call_inverse(width, total_rows, 2, state)
    if by_ring:
        state, ring, beside = lax.optimization_barrier((state, ring, beside))
    while by_ring and len(ring) < outer:
        advance()
    if by_ring:
        beside.append(across_inner(ring[-1]))
    precond = call_inverse(width, total_rows, blocks - 4, (place, *state, turned), last=True)

    if by_ring:
        evals = []
        for arrived, aside in zip(ring, beside):
            evals += [arrived, *aside]
    else:
        evals = [full_eval]
    eval_rows = evals[0].shape[0]
    tile = 256
    return pl.pallas_call(
        score_kernel,
        grid=(eval_rows // tile,),
        out_shape=jax.ShapeDtypeStruct((eval_rows, chip_rows), jnp.bfloat16),
        in_specs=[
            pl.BlockSpec((1, 1, tile), lambda i: (i, 0, 0)),
            pl.BlockSpec((width, chip_rows), lambda i: (0, 0)),
            *[pl.BlockSpec((tile, x.shape[1]), lambda i: (i, 0)) for x in evals],
        ],
        out_specs=pl.BlockSpec((tile, chip_rows), lambda i: (i, 0)),
        compiler_params=pltpu.CompilerParams(vmem_limit_bytes=56 * MIB),
        cost_estimate=pl.CostEstimate(
            flops=2 * eval_rows * width * chip_rows, bytes_accessed=10 * MIB, transcendentals=0
        ),
        name="scores",
    )(eval_bucket.reshape(eval_rows // tile, 1, tile), precond, *evals)


def solution(mesh):
    in_specs = (
        P(("grp", "tr", "ev"), None),
        P(("grp", "ev"), "tr"),
        P(("grp", "ev")),
        P(("grp", "tr", "ev")),
    )
    out_specs = P(("grp", "ev"), "tr")
    return jax.shard_map(shards, mesh=mesh, in_specs=in_specs, out_specs=out_specs, check_vma=False)
```

```python
import functools

import jax
import jax.numpy as jnp
from jax import lax
from jax.experimental import pallas as pl
from jax.experimental.pallas import tpu as pltpu
from jax.sharding import PartitionSpec as P

BUCKETS = 8
BLK = 128
MIB = 2**20

damping = 0.1
weight_table = (0.6, 0.9, 1.3, 1.8, 2.4, 3.1, 3.9, 4.8)

VMEM = pl.BlockSpec(memory_space=pltpu.VMEM)
SMEM = pl.BlockSpec(memory_space=pltpu.SMEM)

def split3(x):
    hi = x.astype(jnp.bfloat16)
    rest = x - hi.astype(jnp.float32)
    mid = rest.astype(jnp.bfloat16)
    low = (rest - mid.astype(jnp.float32)).astype(jnp.bfloat16)
    return hi, mid, low


def as_left(x):
    hi, mid, low = split3(x)
    return jnp.concatenate([hi, mid, hi, mid, hi, low], axis=1)


def as_right(x):
    hi, mid, low = split3(x)
    return jnp.concatenate([hi, hi, mid, mid, low, hi], axis=0)


def mm(left, right):
    return jnp.dot(left, right, preferred_element_type=jnp.float32)


def across(x, lane):
    return jnp.broadcast_to(x[:, lane : lane + 1], x.shape)


def down(x, row):
    return jnp.broadcast_to(x[row : row + 1, :], x.shape)


def total(terms):
    while len(terms) > 1:
        terms = [a + b for a, b in zip(terms[::2], terms[1::2])] + terms[len(terms) & ~1 :]
    return terms[0]


def invert_block(block, beside=()):
    lanes = lax.broadcasted_iota(jnp.int32, (8, BLK), 1)
    subs = lax.broadcasted_iota(jnp.int32, (8, BLK), 0)
    count = BLK // 8
    strips = [block[8 * b : 8 * b + 8, :] for b in range(count)]
    for m in range(count):
        row = strips[m]
        cols = [across(row, 8 * m + t) for t in range(8)]
        for t in range(0, 8, 2):
            first, second = cols[t], cols[t + 1]
            a, b, c = down(first, t), down(second, t), down(second, t + 1)
            scale = 1.0 / (a * c - b * b)
            at_first, at_second = subs == t, subs == t + 1
            own_first, own_second = lanes == 8 * m + t, lanes == 8 * m + t + 1
            upper = jnp.where(own_first, 1.0, jnp.where(own_second, 0.0, down(row, t)))
            lower = jnp.where(own_second, 1.0, jnp.where(own_first, 0.0, down(row, t + 1)))
            lead_first = c * upper - b * lower
            lead_second = a * lower - b * upper
            swept = first * lead_first + second * lead_second
            rest = jnp.where(own_first | own_second, 0.0, row) - swept * scale
            row = jnp.where(at_first, lead_first * scale, jnp.where(at_second, lead_second * scale, rest))
            for s in range(t + 2, 8):
                upper, lower = down(cols[s], t), down(cols[s], t + 1)
                lead_first = c * upper - b * lower
                lead_second = a * lower - b * upper
                swept = first * lead_first + second * lead_second
                cols[s] = jnp.where(
                    at_first,
                    lead_first * scale,
                    jnp.where(at_second, lead_second * scale, cols[s] - swept * scale),
                )
        strips[m] = row
        done = (lanes >= 8 * m) & (lanes < 8 * m + 8)
        leads = [down(row, t) for t in range(8)]
        for b in [*range(m + 1, count), *range(m)]:
            old = strips[b]
            strips[b] = jnp.where(done, 0.0, old) - total([across(old, 8 * m + t) * leads[t] for t in range(8)])
        if m < len(beside):
            beside[m]()
    return jnp.concatenate(strips, axis=0)


def eliminate(src, dst, held, left_ref, right_ref, last=False):
    size = src.shape[0]
    rest = size - BLK
    pivot = held[...]
    scaled = mm(as_left(pivot), as_right(src[0:BLK, BLK:size]))
    left_ref[...] = as_left(src[BLK:size, 0:BLK])
    right_ref[...] = as_right(scaled)
    dst[rest:size, 0:rest] = scaled
    dst[rest:size, rest:size] = pivot

    def strip(top, tall, at, wide):
        def run():
            dst[top : top + tall, at : at + wide] = src[
                BLK + top : BLK + top + tall, BLK + at : BLK + at + wide
            ] - mm(left_ref[top : top + tall, :], right_ref[:, at : at + wide])

        return run

    def border():
        dst[0:rest, rest:size] = -mm(left_ref[...], as_right(pivot))

    wide = 2 * BLK
    work = [strip(0, rest, at, min(wide, rest - at)) for at in range(0, rest, wide)] + [border]
    if last:
        for piece in work:
            piece()
    else:
        ahead = src[BLK : 2 * BLK, BLK : 2 * BLK] - mm(left_ref[0:BLK, :], right_ref[:, 0:BLK])
        spread = []
        for piece in work:
            spread += [piece, lambda: None]
        held[...] = invert_block(ahead, spread)


def gram_kernel(ev_ref, own_ref, other_ref, valid_ref, *refs):
    parts, turned_ref, chip = refs[:-2], refs[-2], refs[-1]
    here = ev_ref[0]
    rows, width = own_ref.shape
    blocks = width // BLK
    half = blocks // 2
    middle = width // 2
    for order, ref in ((here, own_ref), (1 - here, other_ref)):
        at = pl.ds(pl.multiple_of(order * rows, rows), rows)
        for side in range(2):
            to = pl.ds(pl.multiple_of((here + side) % 2 * middle, middle), middle)
            piece = ref[:, side * middle : (side + 1) * middle]
            chip[at, to] = piece
            turned_ref[to, at] = piece.T
    turned_ref[...] = turned_ref[...] * valid_ref[...].astype(jnp.float32).astype(jnp.bfloat16)
    spots = [(ref, at) for ref in parts for at in range(0, ref.shape[0], BLK)]
    for i in range(half):
        part = mm(
            turned_ref[i * BLK : (i + 1) * BLK, :],
            chip[:, i * BLK : (i + half + 1) * BLK],
        )
        for j in range(half + 1):
            ref, at = spots[i * (half + 1) + j]
            ref[at : at + BLK, :] = part[:, j * BLK : (j + 1) * BLK]


def inverse_kernel(total_rows, stages, first, last, *refs):
    if first:
        *parts, matrix_out, held_out, one, two, left_ref, right_ref = refs
    elif last:
        place_ref, matrix_in, held_in, turned_ref, out_ref, one, two, held_out, left_ref, right_ref = refs
    else:
        matrix_in, held_in, matrix_out, held_out, one, two, left_ref, right_ref = refs
    size = one.shape[0]
    blocks = size // BLK
    half = blocks // 2
    if first:
        spots = [(ref, at) for ref in parts for at in range(0, ref.shape[0], BLK)]
        rows = lax.broadcasted_iota(jnp.int32, (BLK, BLK), 0)
        cols = lax.broadcasted_iota(jnp.int32, (BLK, BLK), 1)
        ridge = jnp.where(rows == cols, jnp.float32(damping), 0.0)
        for i in range(blocks):
            for j in range(half + 1):
                ref, at = spots[i * (half + 1) + j]
                c = (i + j) % blocks
                value = ref[at : at + BLK, :] / total_rows
                if j == 0:
                    value = value + ridge
                one[i * BLK : (i + 1) * BLK, c * BLK : (c + 1) * BLK] = value
                if 0 < j < half:
                    one[c * BLK : (c + 1) * BLK, i * BLK : (i + 1) * BLK] = value.T
        held_out[...] = invert_block(one[0:BLK, 0:BLK])
        now = one
    else:
        held_out[...] = held_in[...]
        now = matrix_in
    for stage in range(stages):
        if stage == stages - 1 and not last:
            then = matrix_out
        else:
            then = one if now is two else two
        eliminate(now, then, held_out, left_ref, right_ref, last=last and stage == stages - 1)
        now = then
    if last:
        for i in range(blocks):
            part = mm(now[i * BLK : (i + 1) * BLK, :].astype(jnp.bfloat16), turned_ref[...])
            to = pl.multiple_of(place_ref[i] * BLK, BLK)
            out_ref[pl.ds(to, BLK), :] = part.astype(jnp.bfloat16)


def call_inverse(width, total_rows, stages, operands, first=False, last=False):
    state = (
        jax.ShapeDtypeStruct((width, width), jnp.float32),
        jax.ShapeDtypeStruct((BLK, BLK), jnp.float32),
    )
    result = jax.ShapeDtypeStruct((width, operands[-1].shape[-1]), jnp.bfloat16)
    return pl.pallas_call(
        functools.partial(inverse_kernel, total_rows, stages, first, last),
        out_shape=result if last else state,
        in_specs=[SMEM if x.ndim == 1 else VMEM for x in operands],
        out_specs=VMEM if last else (VMEM, VMEM),
        scratch_shapes=[
            pltpu.VMEM((width, width), jnp.float32),
            pltpu.VMEM((width, width), jnp.float32),
            *([pltpu.VMEM((BLK, BLK), jnp.float32)] if last else []),
            pltpu.VMEM((width - BLK, 6 * BLK), jnp.bfloat16),
            pltpu.VMEM((6 * BLK, width - BLK), jnp.bfloat16),
        ],
        compiler_params=pltpu.CompilerParams(vmem_limit_bytes=36 * MIB),
        cost_estimate=pl.CostEstimate(flops=stages * 6_000_000_000, bytes_accessed=4 * MIB, transcendentals=0),
        name="inverse",
    )(*operands)


def score_kernel(halves, bucket_ref, precond_ref, *refs):
    *eval_refs, out_ref = refs
    width = precond_ref.shape[0]
    bucket = bucket_ref[0]
    weight = jnp.zeros(bucket.shape, jnp.float32)
    for level in range(BUCKETS):
        weight = weight + jnp.where(bucket == level, jnp.float32(weight_table[level]), 0.0)
    weight = weight / jnp.sqrt(jnp.float32(width))
    rows = out_ref.shape[0]
    evals = []
    for count in halves:
        some, eval_refs = eval_refs[:count], eval_refs[count:]
        value = some[0][...]
        if count == 2:
            value = jnp.where(pl.program_id(0) < pl.num_programs(0) // 2, value, some[1][...])
        evals.append(value)
    evals = jnp.concatenate(evals, axis=1)
    scores = mm(evals, precond_ref[...])
    for at in range(0, rows, BLK):
        factor = jnp.broadcast_to(weight[:, at : at + BLK], (BLK, BLK)).T
        for to in range(0, out_ref.shape[1], BLK):
            out_ref[at : at + BLK, to : to + BLK] = (
                scores[at : at + BLK, to : to + BLK] * factor
            ).astype(jnp.bfloat16)


def shift(members, stride, by):
    n = lax.axis_size("tr")
    pairs = []
    for i in range(n):
        p = i // stride % members
        pairs.append((i, i + ((p + by) % members - p) * stride))
    return pairs


def scatter_sum(x, members, stride):
    me = lax.axis_index("tr") // stride % members
    chunks = x.reshape(members, -1, BLK)
    mine = lax.dynamic_index_in_dim(chunks, me, keepdims=False)
    got = [
        lax.ppermute(
            lax.dynamic_index_in_dim(chunks, (me + by) % members, keepdims=False), "tr", shift(members, stride, by)
        )
        for by in range(1, members)
    ]
    for piece in got:
        mine = mine + piece
    return mine


def collect(x, members, stride):
    me = lax.axis_index("tr") // stride % members
    got = [x] + [lax.ppermute(x, "tr", shift(members, stride, by)) for by in range(members - 1, 0, -1)]
    if members == 2:
        whole = jnp.where(
            me == 0, jnp.concatenate(got, axis=0), jnp.concatenate(got[::-1], axis=0)
        )
        return whole
    twice = jnp.concatenate(got + got, axis=0)
    return lax.dynamic_slice_in_dim(twice, (members - me) * x.shape[0], members * x.shape[0])


def chip_axes():
    n = lax.axis_size("tr")
    inner = 2 ** ((n.bit_length() - 1) // 2)
    return (inner, 1), (n // inner, inner)


def sum_over_tr(parts):
    axes = chip_axes()
    orders = [axes, axes[::-1]]
    parts = [scatter_sum(x, *order[0]) for x, order in zip(parts, orders)]
    parts = [scatter_sum(x, *order[1]) for x, order in zip(parts, orders)]
    parts = [collect(x, *order[1]) for x, order in zip(parts, orders)]
    return [collect(x, *order[0]) for x, order in zip(parts, orders)]


def shards(train_grads, eval_grads, eval_bucket, train_valid):
    rows_here, width = train_grads.shape
    total_rows = rows_here * lax.axis_size("tr") * lax.axis_size("ev")
    here = lax.axis_index("ev")
    tr = lax.axis_index("tr")
    swap = [(0, 1), (1, 0)]
    blocks = width // BLK
    half = blocks // 2
    (inner, _), (outer, _) = chip_axes()
    by_ring = eval_grads.shape[1] % BLK == 0

    def across_inner(x):
        return [lax.ppermute(x, "tr", shift(inner, 1, by)) for by in range(1, inner)]

    def along_outer(x):
        return lax.ppermute(x, "tr", shift(outer, inner, 1))

    other_train = lax.ppermute(train_grads, "ev", swap)
    other_valid = lax.ppermute(train_valid, "ev", swap)
    chip_valid = jnp.where(
        here == 0, jnp.concatenate([train_valid, other_valid]), jnp.concatenate([other_valid, train_valid])
    )
    chip_rows = 2 * rows_here
    held = half * (half + 1) * BLK
    first_held = half * (half + 1) * 13 // 20 * BLK
    *local_gram, turned = pl.pallas_call(
        gram_kernel,
        out_shape=(
            jax.ShapeDtypeStruct((first_held, BLK), jnp.float32),
            jax.ShapeDtypeStruct((held - first_held, BLK), jnp.float32),
            jax.ShapeDtypeStruct((width, chip_rows), jnp.bfloat16),
        ),
        in_specs=[SMEM, VMEM, VMEM, VMEM],
        out_specs=(VMEM,) * 3,
        scratch_shapes=[pltpu.VMEM((chip_rows, width), jnp.bfloat16)],
        compiler_params=pltpu.CompilerParams(vmem_limit_bytes=32 * MIB),
        cost_estimate=pl.CostEstimate(flops=2 * chip_rows * held * BLK, bytes_accessed=6 * MIB, transcendentals=0),
        name="gram",
    )(here.reshape(1), train_grads, other_train, chip_valid[None, :])

    ring = [eval_grads]
    beside = []
    if by_ring:
        ring.append(along_outer(eval_grads))
        beside.append(across_inner(eval_grads))
        local_gram, ring, beside = lax.optimization_barrier((local_gram, ring, beside))

    own_gram = sum_over_tr(local_gram)
    other_gram = [lax.ppermute(x, "ev", swap) for x in own_gram]
    gram = [*own_gram, *other_gram]

    column = (jnp.arange(blocks, dtype=jnp.int32) + half * here) % blocks
    if by_ring:
        gram, ring, beside = lax.optimization_barrier((gram, ring, beside))
        owner = column * BLK // eval_grads.shape[1]
        behind = (tr // inner - owner // inner) % outer
        aside = (tr - owner) % inner
        each = eval_grads.shape[1] // BLK
        place = (behind * inner + aside) * each + column % each
    else:
        gram, eval_grads = lax.optimization_barrier((gram, eval_grads))
        full_eval = lax.all_gather(eval_grads, "tr", axis=1, tiled=True)
        place = column

    def advance():
        if by_ring and len(ring) < outer:
            arrived = ring[-1]
            ring.append(along_outer(arrived))
            beside.append(across_inner(arrived))

    advance()
    state = call_inverse(width, total_rows, 2, gram, first=True)
    if by_ring:
        state, ring, beside = lax.optimization_barrier((state, ring, beside))
    advance()
    state = call_inverse(width, total_rows, 3, state)
    if by_ring:
        state, ring, beside = lax.optimization_barrier((state, ring, beside))
        while len(ring) < outer:
            advance()
        evals = []
        for arrived, aside in zip(ring, beside):
            evals.append([arrived])
            evals += [[x] for x in aside]
        rows = ring[-1].shape[0] // 2
        for by, before in enumerate(beside[-1], 1):
            top = lax.ppermute(ring[-1][:rows], "tr", shift(inner, 1, by))
            low = along_outer(before[rows:])
            if by == 1:
                evals.append([ring[-1]])
            evals.append([top, low])
    else:
        evals = [[full_eval]]
    precond = call_inverse(width, total_rows, blocks - 5, (place, *state, turned), last=True)

    eval_rows = sum(x.shape[0] for x in evals[0])
    tile = 512
    tiles = eval_rows // tile
    pieces = [x for block in evals for x in block]
    halves = [len(block) for block in evals]
    specs = []
    for block in evals:
        for n, x in enumerate(block):
            each = tiles // len(block)
            specs.append(
                pl.BlockSpec((tile, x.shape[1]), lambda i, low=n * each, each=each: (jnp.clip(i - low, 0, each - 1), 0))
            )
    return pl.pallas_call(
        functools.partial(score_kernel, halves),
        grid=(eval_rows // tile,),
        out_shape=jax.ShapeDtypeStruct((eval_rows, chip_rows), jnp.bfloat16),
        in_specs=[
            pl.BlockSpec((1, 1, tile), lambda i: (i, 0, 0)),
            pl.BlockSpec((width, chip_rows), lambda i: (0, 0)),
            *specs,
        ],
        out_specs=pl.BlockSpec((tile, chip_rows), lambda i: (i, 0)),
        compiler_params=pltpu.CompilerParams(vmem_limit_bytes=24 * MIB),
        cost_estimate=pl.CostEstimate(
            flops=2 * eval_rows * width * chip_rows, bytes_accessed=10 * MIB, transcendentals=0
        ),
        name="scores",
    )(eval_bucket.reshape(eval_rows // tile, 1, tile), precond, *pieces)


def solution(mesh):
    in_specs = (
        P(("grp", "tr", "ev"), None),
        P(("grp", "ev"), "tr"),
        P(("grp", "ev")),
        P(("grp", "tr", "ev")),
    )
    out_specs = P(("grp", "ev"), "tr")
    return jax.shard_map(shards, mesh=mesh, in_specs=in_specs, out_specs=out_specs, check_vma=False)
```

```python
import functools

import jax
import jax.numpy as jnp
from jax import lax
from jax.experimental import pallas as pl
from jax.experimental.pallas import tpu as pltpu
from jax.sharding import PartitionSpec as P

BUCKETS = 8
BLK = 128
MIB = 2**20

damping = 0.1
weight_table = (0.6, 0.9, 1.3, 1.8, 2.4, 3.1, 3.9, 4.8)

VMEM = pl.BlockSpec(memory_space=pltpu.VMEM)
SMEM = pl.BlockSpec(memory_space=pltpu.SMEM)

def split3(x):
    hi = x.astype(jnp.bfloat16)
    rest = x - hi.astype(jnp.float32)
    mid = rest.astype(jnp.bfloat16)
    low = (rest - mid.astype(jnp.float32)).astype(jnp.bfloat16)
    return hi, mid, low


def as_left(x):
    hi, mid, low = split3(x)
    return jnp.concatenate([hi, mid, hi, mid, hi, low], axis=1)


def as_right(x):
    hi, mid, low = split3(x)
    return jnp.concatenate([hi, hi, mid, mid, low, hi], axis=0)


def mm(left, right):
    return jnp.dot(left, right, preferred_element_type=jnp.float32)


def across(x, lane):
    return jnp.broadcast_to(x[:, lane : lane + 1], x.shape)


def down(x, row):
    return jnp.broadcast_to(x[row : row + 1, :], x.shape)


def total(terms):
    while len(terms) > 1:
        terms = [a + b for a, b in zip(terms[::2], terms[1::2])] + terms[len(terms) & ~1 :]
    return terms[0]


def invert_block(block, beside=()):
    lanes = lax.broadcasted_iota(jnp.int32, (8, BLK), 1)
    subs = lax.broadcasted_iota(jnp.int32, (8, BLK), 0)
    count = BLK // 8
    strips = [block[8 * b : 8 * b + 8, :] for b in range(count)]
    for m in range(count):
        row = strips[m]
        cols = [across(row, 8 * m + t) for t in range(8)]
        for t in range(0, 8, 2):
            first, second = cols[t], cols[t + 1]
            a, b, c = down(first, t), down(second, t), down(second, t + 1)
            scale = 1.0 / (a * c - b * b)
            at_first, at_second = subs == t, subs == t + 1
            own_first, own_second = lanes == 8 * m + t, lanes == 8 * m + t + 1
            upper = jnp.where(own_first, 1.0, jnp.where(own_second, 0.0, down(row, t)))
            lower = jnp.where(own_second, 1.0, jnp.where(own_first, 0.0, down(row, t + 1)))
            lead_first = c * upper - b * lower
            lead_second = a * lower - b * upper
            swept = first * lead_first + second * lead_second
            rest = jnp.where(own_first | own_second, 0.0, row) - swept * scale
            row = jnp.where(at_first, lead_first * scale, jnp.where(at_second, lead_second * scale, rest))
            for s in range(t + 2, 8):
                upper, lower = down(cols[s], t), down(cols[s], t + 1)
                lead_first = c * upper - b * lower
                lead_second = a * lower - b * upper
                swept = first * lead_first + second * lead_second
                cols[s] = jnp.where(
                    at_first,
                    lead_first * scale,
                    jnp.where(at_second, lead_second * scale, cols[s] - swept * scale),
                )
        strips[m] = row
        for piece in beside[m * len(beside) // count : (m + 1) * len(beside) // count]:
            piece()
        done = (lanes >= 8 * m) & (lanes < 8 * m + 8)
        leads = [down(row, t) for t in range(8)]
        for b in [*range(m + 1, count), *range(m)]:
            old = strips[b]
            strips[b] = jnp.where(done, 0.0, old) - total([across(old, 8 * m + t) * leads[t] for t in range(8)])
    return jnp.concatenate(strips, axis=0)


def eliminate(src, dst, held, left_ref, right_ref, last=False):
    size = src.shape[0]
    rest = size - BLK
    pivot = held[...]
    scaled = mm(as_left(pivot), as_right(src[0:BLK, BLK:size]))
    left_ref[...] = as_left(src[BLK:size, 0:BLK])
    right_ref[...] = as_right(scaled)
    dst[rest:size, 0:rest] = scaled
    dst[rest:size, rest:size] = pivot

    def strip(top, tall, at, wide):
        def run():
            dst[top : top + tall, at : at + wide] = src[
                BLK + top : BLK + top + tall, BLK + at : BLK + at + wide
            ] - mm(left_ref[top : top + tall, :], right_ref[:, at : at + wide])

        return run

    def border():
        dst[0:rest, rest:size] = -mm(left_ref[...], as_right(pivot))

    wide = 2 * BLK
    tall = rest if last else rest // 2
    work = [
        strip(top, tall, at, min(wide, rest - at)) for at in range(0, rest, wide) for top in range(0, rest, tall)
    ] + [border]
    if last:
        for piece in work:
            piece()
    else:
        ahead = src[BLK : 2 * BLK, BLK : 2 * BLK] - mm(left_ref[0:BLK, :], right_ref[:, 0:BLK])
        held[...] = invert_block(ahead, work)


def gram_kernel(ev_ref, own_ref, other_ref, valid_ref, *refs):
    parts, turned_ref, chip = refs[:-2], refs[-2], refs[-1]
    here = ev_ref[0]
    rows, width = own_ref.shape
    blocks = width // BLK
    half = blocks // 2
    middle = width // 2
    for order, ref in ((here, own_ref), (1 - here, other_ref)):
        at = pl.ds(pl.multiple_of(order * rows, rows), rows)
        for side in range(2):
            to = pl.ds(pl.multiple_of((here + side) % 2 * middle, middle), middle)
            piece = ref[:, side * middle : (side + 1) * middle]
            chip[at, to] = piece
            turned_ref[to, at] = piece.T
    turned_ref[...] = turned_ref[...] * valid_ref[...].astype(jnp.float32).astype(jnp.bfloat16)
    spots = [(ref, at) for ref in parts for at in range(0, ref.shape[0], BLK)]
    for i in range(half):
        part = mm(
            turned_ref[i * BLK : (i + 1) * BLK, :],
            chip[:, i * BLK : (i + half + 1) * BLK],
        )
        for j in range(half + 1):
            ref, at = spots[i * (half + 1) + j]
            ref[at : at + BLK, :] = part[:, j * BLK : (j + 1) * BLK]


def inverse_kernel(total_rows, stages, first, last, *refs):
    if first:
        *parts, matrix_out, held_out, one, two, left_ref, right_ref = refs
    elif last:
        place_ref, matrix_in, held_in, turned_ref, out_ref, one, two, held_out, placed, left_ref, right_ref = refs
    else:
        matrix_in, held_in, matrix_out, held_out, one, two, left_ref, right_ref = refs
    size = one.shape[0]
    blocks = size // BLK
    half = blocks // 2
    if first:
        spots = [(ref, at) for ref in parts for at in range(0, ref.shape[0], BLK)]
        rows = lax.broadcasted_iota(jnp.int32, (BLK, BLK), 0)
        cols = lax.broadcasted_iota(jnp.int32, (BLK, BLK), 1)
        ridge = jnp.where(rows == cols, jnp.float32(damping), 0.0)
        for i in range(blocks):
            for j in range(half + 1):
                ref, at = spots[i * (half + 1) + j]
                c = (i + j) % blocks
                value = ref[at : at + BLK, :] / total_rows
                if j == 0:
                    value = value + ridge
                one[i * BLK : (i + 1) * BLK, c * BLK : (c + 1) * BLK] = value
                if 0 < j < half:
                    one[c * BLK : (c + 1) * BLK, i * BLK : (i + 1) * BLK] = value.T
        held_out[...] = invert_block(one[0:BLK, 0:BLK])
        now = one
    else:
        held_out[...] = held_in[...]
        now = matrix_in
    for stage in range(stages):
        if stage == stages - 1 and not last:
            then = matrix_out
        else:
            then = one if now is two else two
        eliminate(now, then, held_out, left_ref, right_ref, last=last and stage == stages - 1)
        now = then
    if last:
        for i in range(blocks):
            to = pl.multiple_of(place_ref[i] * BLK, BLK)
            placed[pl.ds(to, BLK), :] = now[i * BLK : (i + 1) * BLK, :].astype(jnp.bfloat16)
        wide = 2 * BLK
        for at in range(0, out_ref.shape[1], wide):
            out_ref[:, at : at + wide] = mm(placed[...], turned_ref[:, at : at + wide]).astype(jnp.bfloat16)


def call_inverse(width, total_rows, stages, operands, first=False, last=False):
    state = (
        jax.ShapeDtypeStruct((width, width), jnp.float32),
        jax.ShapeDtypeStruct((BLK, BLK), jnp.float32),
    )
    result = jax.ShapeDtypeStruct((width, operands[-1].shape[-1]), jnp.bfloat16)
    return pl.pallas_call(
        functools.partial(inverse_kernel, total_rows, stages, first, last),
        out_shape=result if last else state,
        in_specs=[SMEM if x.ndim == 1 else VMEM for x in operands],
        out_specs=VMEM if last else (VMEM, VMEM),
        scratch_shapes=[
            pltpu.VMEM((width, width), jnp.float32),
            pltpu.VMEM((width, width), jnp.float32),
            *([pltpu.VMEM((BLK, BLK), jnp.float32), pltpu.VMEM((width, width), jnp.bfloat16)] if last else []),
            pltpu.VMEM((width - BLK, 6 * BLK), jnp.bfloat16),
            pltpu.VMEM((6 * BLK, width - BLK), jnp.bfloat16),
        ],
        compiler_params=pltpu.CompilerParams(vmem_limit_bytes=36 * MIB),
        cost_estimate=pl.CostEstimate(flops=stages * 6_000_000_000, bytes_accessed=4 * MIB, transcendentals=0),
        name="inverse",
    )(*operands)


def score_kernel(halves, bucket_ref, precond_ref, *refs):
    *eval_refs, out_ref = refs
    width = precond_ref.shape[0]
    bucket = bucket_ref[0]
    weight = jnp.zeros(bucket.shape, jnp.float32)
    for level in range(BUCKETS):
        weight = weight + jnp.where(bucket == level, jnp.float32(weight_table[level]), 0.0)
    weight = weight / jnp.sqrt(jnp.float32(width))
    rows = out_ref.shape[0]
    evals = []
    for count in halves:
        some, eval_refs = eval_refs[:count], eval_refs[count:]
        value = some[0][...]
        if count == 2:
            value = jnp.where(pl.program_id(0) < pl.num_programs(0) // 2, value, some[1][...])
        evals.append(value)
    evals = jnp.concatenate(evals, axis=1)
    scores = mm(evals, precond_ref[...])
    for at in range(0, rows, BLK):
        factor = jnp.broadcast_to(weight[:, at : at + BLK], (BLK, BLK)).T
        for to in range(0, out_ref.shape[1], BLK):
            out_ref[at : at + BLK, to : to + BLK] = (
                scores[at : at + BLK, to : to + BLK] * factor
            ).astype(jnp.bfloat16)


def shift(members, stride, by):
    n = lax.axis_size("tr")
    pairs = []
    for i in range(n):
        p = i // stride % members
        pairs.append((i, i + ((p + by) % members - p) * stride))
    return pairs


def scatter_sum(x, members, stride):
    me = lax.axis_index("tr") // stride % members
    chunks = x.reshape(members, -1, BLK)
    mine = lax.dynamic_index_in_dim(chunks, me, keepdims=False)
    got = [
        lax.ppermute(
            lax.dynamic_index_in_dim(chunks, (me + by) % members, keepdims=False), "tr", shift(members, stride, by)
        )
        for by in range(1, members)
    ]
    for piece in got:
        mine = mine + piece
    return mine


def collect(x, members, stride):
    me = lax.axis_index("tr") // stride % members
    got = [x] + [lax.ppermute(x, "tr", shift(members, stride, by)) for by in range(members - 1, 0, -1)]
    if members == 2:
        whole = jnp.where(
            me == 0, jnp.concatenate(got, axis=0), jnp.concatenate(got[::-1], axis=0)
        )
        return whole
    twice = jnp.concatenate(got + got, axis=0)
    return lax.dynamic_slice_in_dim(twice, (members - me) * x.shape[0], members * x.shape[0])


def chip_axes():
    n = lax.axis_size("tr")
    inner = 2 ** ((n.bit_length() - 1) // 2)
    return (inner, 1), (n // inner, inner)


def sum_over_tr(parts):
    axes = chip_axes()
    orders = [axes, axes[::-1]]
    parts = [scatter_sum(x, *order[0]) for x, order in zip(parts, orders)]
    parts = [scatter_sum(x, *order[1]) for x, order in zip(parts, orders)]
    parts = lax.optimization_barrier([collect(x, *order[1]) for x, order in zip(parts, orders)])
    return [collect(x, *order[0]) for x, order in zip(parts, orders)]


def shards(train_grads, eval_grads, eval_bucket, train_valid):
    rows_here, width = train_grads.shape
    total_rows = rows_here * lax.axis_size("tr") * lax.axis_size("ev")
    here = lax.axis_index("ev")
    tr = lax.axis_index("tr")
    swap = [(0, 1), (1, 0)]
    blocks = width // BLK
    half = blocks // 2
    (inner, _), (outer, _) = chip_axes()
    by_ring = eval_grads.shape[1] % BLK == 0

    def across_inner(x):
        return [lax.ppermute(x, "tr", shift(inner, 1, by)) for by in range(1, inner)]

    def along_outer(x):
        return lax.ppermute(x, "tr", shift(outer, inner, 1))

    other_train = lax.ppermute(train_grads, "ev", swap)
    other_valid = lax.ppermute(train_valid, "ev", swap)
    chip_valid = jnp.where(
        here == 0, jnp.concatenate([train_valid, other_valid]), jnp.concatenate([other_valid, train_valid])
    )
    chip_rows = 2 * rows_here
    held = half * (half + 1) * BLK
    first_held = half * (half + 1) * 13 // 20 * BLK
    *local_gram, turned = pl.pallas_call(
        gram_kernel,
        out_shape=(
            jax.ShapeDtypeStruct((first_held, BLK), jnp.float32),
            jax.ShapeDtypeStruct((held - first_held, BLK), jnp.float32),
            jax.ShapeDtypeStruct((width, chip_rows), jnp.bfloat16),
        ),
        in_specs=[SMEM, VMEM, VMEM, VMEM],
        out_specs=(VMEM,) * 3,
        scratch_shapes=[pltpu.VMEM((chip_rows, width), jnp.bfloat16)],
        compiler_params=pltpu.CompilerParams(vmem_limit_bytes=32 * MIB),
        cost_estimate=pl.CostEstimate(flops=2 * chip_rows * held * BLK, bytes_accessed=6 * MIB, transcendentals=0),
        name="gram",
    )(here.reshape(1), train_grads, other_train, chip_valid[None, :])

    ring = [eval_grads]
    beside = []
    if by_ring:
        ring.append(along_outer(eval_grads))
        beside.append(across_inner(eval_grads))
        local_gram, ring, beside = lax.optimization_barrier((local_gram, ring, beside))

    own_gram = sum_over_tr(local_gram)
    other_gram = [lax.ppermute(x, "ev", swap) for x in own_gram]
    gram = [*own_gram, *other_gram]

    column = (jnp.arange(blocks, dtype=jnp.int32) + half * here) % blocks
    if by_ring:
        gram, ring, beside = lax.optimization_barrier((gram, ring, beside))
        owner = column * BLK // eval_grads.shape[1]
        behind = (tr // inner - owner // inner) % outer
        aside = (tr - owner) % inner
        each = eval_grads.shape[1] // BLK
        place = (behind * inner + aside) * each + column % each
    else:
        gram, eval_grads = lax.optimization_barrier((gram, eval_grads))
        full_eval = lax.all_gather(eval_grads, "tr", axis=1, tiled=True)
        place = column

    def advance():
        if by_ring and len(ring) < outer:
            arrived = ring[-1]
            ring.append(along_outer(arrived))
            beside.append(across_inner(arrived))

    advance()
    state = call_inverse(width, total_rows, 2, gram, first=True)
    if by_ring:
        state, ring, beside = lax.optimization_barrier((state, ring, beside))
    advance()
    state = call_inverse(width, total_rows, 3, state)
    if by_ring:
        state, ring, beside = lax.optimization_barrier((state, ring, beside))
        while len(ring) < outer:
            advance()
        evals = []
        for arrived, aside in zip(ring, beside):
            evals.append([arrived])
            evals += [[x] for x in aside]
        rows = ring[-1].shape[0] // 2
        for by, before in enumerate(beside[-1], 1):
            top = lax.ppermute(ring[-1][:rows], "tr", shift(inner, 1, by))
            low = along_outer(before[rows:])
            if by == 1:
                evals.append([ring[-1]])
            evals.append([top, low])
    else:
        evals = [[full_eval]]
    precond = call_inverse(width, total_rows, blocks - 5, (place, *state, turned), last=True)

    eval_rows = sum(x.shape[0] for x in evals[0])
    tile = 512
    tiles = eval_rows // tile
    pieces = [x for block in evals for x in block]
    halves = [len(block) for block in evals]
    specs = []
    for block in evals:
        for n, x in enumerate(block):
            each = tiles // len(block)
            specs.append(
                pl.BlockSpec((tile, x.shape[1]), lambda i, low=n * each, each=each: (jnp.clip(i - low, 0, each - 1), 0))
            )
    return pl.pallas_call(
        functools.partial(score_kernel, halves),
        grid=(eval_rows // tile,),
        out_shape=jax.ShapeDtypeStruct((eval_rows, chip_rows), jnp.bfloat16),
        in_specs=[
            pl.BlockSpec((1, 1, tile), lambda i: (i, 0, 0)),
            pl.BlockSpec((width, chip_rows), lambda i: (0, 0)),
            *specs,
        ],
        out_specs=pl.BlockSpec((tile, chip_rows), lambda i: (i, 0)),
        compiler_params=pltpu.CompilerParams(vmem_limit_bytes=24 * MIB),
        cost_estimate=pl.CostEstimate(
            flops=2 * eval_rows * width * chip_rows, bytes_accessed=10 * MIB, transcendentals=0
        ),
        name="scores",
    )(eval_bucket.reshape(eval_rows // tile, 1, tile), precond, *pieces)


def solution(mesh):
    in_specs = (
        P(("grp", "tr", "ev"), None),
        P(("grp", "ev"), "tr"),
        P(("grp", "ev")),
        P(("grp", "tr", "ev")),
    )
    out_specs = P(("grp", "ev"), "tr")
    return jax.shard_map(shards, mesh=mesh, in_specs=in_specs, out_specs=out_specs, check_vma=False)
```

```python
import functools

import jax
import jax.numpy as jnp
from jax import lax
from jax.experimental import pallas as pl
from jax.experimental.pallas import tpu as pltpu
from jax.sharding import PartitionSpec as P

BUCKETS = 8
BLK = 128
MIB = 2**20

damping = 0.1
weight_table = (0.6, 0.9, 1.3, 1.8, 2.4, 3.1, 3.9, 4.8)

VMEM = pl.BlockSpec(memory_space=pltpu.VMEM)
SMEM = pl.BlockSpec(memory_space=pltpu.SMEM)

def split3(x):
    hi = x.astype(jnp.bfloat16)
    rest = x - hi.astype(jnp.float32)
    mid = rest.astype(jnp.bfloat16)
    low = (rest - mid.astype(jnp.float32)).astype(jnp.bfloat16)
    return hi, mid, low


def as_left(x):
    hi, mid, low = split3(x)
    return jnp.concatenate([hi, mid, hi, mid, hi, low], axis=1)


def as_right(x):
    hi, mid, low = split3(x)
    return jnp.concatenate([hi, hi, mid, mid, low, hi], axis=0)


def mm(left, right):
    return jnp.dot(left, right, preferred_element_type=jnp.float32)


def across(x, lane):
    return jnp.broadcast_to(x[:, lane : lane + 1], x.shape)


def down(x, row):
    return jnp.broadcast_to(x[row : row + 1, :], x.shape)


def total(terms):
    while len(terms) > 1:
        terms = [a + b for a, b in zip(terms[::2], terms[1::2])] + terms[len(terms) & ~1 :]
    return terms[0]


def invert_block(block, beside=()):
    lanes = lax.broadcasted_iota(jnp.int32, (8, BLK), 1)
    subs = lax.broadcasted_iota(jnp.int32, (8, BLK), 0)
    count = BLK // 8
    strips = [block[8 * b : 8 * b + 8, :] for b in range(count)]
    for m in range(count):
        row = strips[m]
        cols = [across(row, 8 * m + t) for t in range(8)]
        for t in range(0, 8, 2):
            first, second = cols[t], cols[t + 1]
            a, b, c = down(first, t), down(second, t), down(second, t + 1)
            scale = 1.0 / (a * c - b * b)
            at_first, at_second = subs == t, subs == t + 1
            own_first, own_second = lanes == 8 * m + t, lanes == 8 * m + t + 1
            upper = jnp.where(own_first, 1.0, jnp.where(own_second, 0.0, down(row, t)))
            lower = jnp.where(own_second, 1.0, jnp.where(own_first, 0.0, down(row, t + 1)))
            lead_first = c * upper - b * lower
            lead_second = a * lower - b * upper
            swept = first * lead_first + second * lead_second
            rest = jnp.where(own_first | own_second, 0.0, row) - swept * scale
            row = jnp.where(at_first, lead_first * scale, jnp.where(at_second, lead_second * scale, rest))
            for s in range(t + 2, 8):
                upper, lower = down(cols[s], t), down(cols[s], t + 1)
                lead_first = c * upper - b * lower
                lead_second = a * lower - b * upper
                swept = first * lead_first + second * lead_second
                cols[s] = jnp.where(
                    at_first,
                    lead_first * scale,
                    jnp.where(at_second, lead_second * scale, cols[s] - swept * scale),
                )
        strips[m] = row
        for piece in beside[m * len(beside) // count : (m + 1) * len(beside) // count]:
            piece()
        done = (lanes >= 8 * m) & (lanes < 8 * m + 8)
        leads = [down(row, t) for t in range(8)]
        for b in [*range(m + 1, count), *range(m)]:
            old = strips[b]
            strips[b] = jnp.where(done, 0.0, old) - total([across(old, 8 * m + t) * leads[t] for t in range(8)])
    return jnp.concatenate(strips, axis=0)


def eliminate(done, src, dst, held, left_ref, right_ref, last=False):
    size = src.shape[0]
    rest = size - BLK
    pivot = held[...]
    right_ref[...] = as_right(mm(as_left(pivot), as_right(src[0:BLK, BLK:size])))
    for at in range(BLK, size, BLK):
        turned = src[0:BLK, at : at + BLK].T
        left_ref[at - BLK : at, :] = as_left(-turned if at >= size - done * BLK else turned)
    dst[rest:size, rest:size] = pivot

    def strip(top, tall, at, wide):
        def run():
            dst[top : top + tall, at : at + wide] = src[
                BLK + top : BLK + top + tall, BLK + at : BLK + at + wide
            ] - mm(left_ref[top : top + tall, :], right_ref[:, at : at + wide])

        return run

    def border():
        dst[0:rest, rest:size] = -mm(left_ref[...], as_right(pivot))

    wide = 2 * BLK
    work = []
    for at in range(0, rest, wide):
        n = min(wide, rest - at)
        work.append(strip(0, at + n, at, n))
    work.append(border)
    if last:
        for piece in work:
            piece()
    else:
        ahead = src[BLK : 2 * BLK, BLK : 2 * BLK] - mm(left_ref[0:BLK, :], right_ref[:, 0:BLK])
        held[...] = invert_block(ahead, work)


def gram_kernel(ev_ref, own_ref, other_ref, valid_ref, *refs):
    parts, turned_ref, chip = refs[:-2], refs[-2], refs[-1]
    here = ev_ref[0]
    rows, width = own_ref.shape
    blocks = width // BLK
    half = blocks // 2
    middle = width // 2
    for order, ref in ((here, own_ref), (1 - here, other_ref)):
        at = pl.ds(pl.multiple_of(order * rows, rows), rows)
        for side in range(2):
            to = pl.ds(pl.multiple_of((here + side) % 2 * middle, middle), middle)
            piece = ref[:, side * middle : (side + 1) * middle]
            chip[at, to] = piece
            turned_ref[to, at] = piece.T
    turned_ref[...] = turned_ref[...] * valid_ref[...].astype(jnp.float32).astype(jnp.bfloat16)
    spots = [(ref, at) for ref in parts for at in range(0, ref.shape[0], BLK)]
    for i in range(half):
        part = mm(
            turned_ref[i * BLK : (i + 1) * BLK, :],
            chip[:, i * BLK : (i + half) * BLK],
        )
        for j in range(half):
            ref, at = spots[i * half + j]
            ref[at : at + BLK, :] = part[:, j * BLK : (j + 1) * BLK]
    for t in range(half // 2):
        i = here * (half // 2) + t
        ref, at = spots[half * half + t]
        ref[at : at + BLK, :] = mm(
            turned_ref[pl.ds(pl.multiple_of(i * BLK, BLK), BLK), :],
            chip[:, pl.ds(pl.multiple_of((i + half) * BLK, BLK), BLK)],
        )


def inverse_kernel(total_rows, start, stages, first, last, *refs):
    if first:
        ev_ref, *parts, matrix_out, held_out, one, two, left_ref, right_ref = refs
    elif last:
        place_ref, matrix_in, held_in, turned_ref, out_ref, one, two, held_out, placed, left_ref, right_ref = refs
    else:
        matrix_in, held_in, matrix_out, held_out, one, two, left_ref, right_ref = refs
    size = one.shape[0]
    blocks = size // BLK
    half = blocks // 2
    if first:
        spots = [(ref, at) for ref in parts for at in range(0, ref.shape[0], BLK)]
        rows = lax.broadcasted_iota(jnp.int32, (BLK, BLK), 0)
        cols = lax.broadcasted_iota(jnp.int32, (BLK, BLK), 1)
        ridge = jnp.where(rows == cols, jnp.float32(damping), 0.0)
        count = len(spots) // 2
        for i in range(blocks):
            for j in range(half):
                ref, at = spots[i // half * count + i % half * half + j]
                c = (i + j) % blocks
                value = ref[at : at + BLK, :] / total_rows
                if j == 0:
                    value = value + ridge
                if c < i:
                    i_to, c_to, value = c, i, value.T
                else:
                    i_to, c_to = i, c
                one[i_to * BLK : (i_to + 1) * BLK, c_to * BLK : (c_to + 1) * BLK] = value
        for side in range(2):
            for t in range(half // 2):
                ref, at = spots[side * count + half * half + t]
                i = (ev_ref[0] + side) % 2 * (half // 2) + t
                value = ref[at : at + BLK, :] / total_rows
                one[
                    pl.ds(pl.multiple_of(i * BLK, BLK), BLK),
                    pl.ds(pl.multiple_of((i + half) * BLK, BLK), BLK),
                ] = value.T if side else value
        held_out[...] = invert_block(one[0:BLK, 0:BLK])
        now = one
    else:
        held_out[...] = held_in[...]
        now = matrix_in
    for stage in range(stages):
        if stage == stages - 1 and not last:
            then = matrix_out
        else:
            then = one if now is two else two
        eliminate(start + stage, now, then, held_out, left_ref, right_ref, last=last and stage == stages - 1)
        now = then
    if last:
        for i in range(blocks):
            to = pl.ds(pl.multiple_of(place_ref[i] * BLK, BLK), BLK)
            for j in range(blocks):
                value = now[min(i, j) * BLK : (min(i, j) + 1) * BLK, max(i, j) * BLK : (max(i, j) + 1) * BLK]
                value = value.astype(jnp.bfloat16)
                placed[to, j * BLK : (j + 1) * BLK] = value.T if j < i else value
        wide = 2 * BLK
        for at in range(0, out_ref.shape[1], wide):
            out_ref[:, at : at + wide] = mm(placed[...], turned_ref[:, at : at + wide]).astype(jnp.bfloat16)


def call_inverse(width, total_rows, start, stages, operands, first=False, last=False):
    state = (
        jax.ShapeDtypeStruct((width, width), jnp.float32),
        jax.ShapeDtypeStruct((BLK, BLK), jnp.float32),
    )
    result = jax.ShapeDtypeStruct((width, operands[-1].shape[-1]), jnp.bfloat16)
    return pl.pallas_call(
        functools.partial(inverse_kernel, total_rows, start, stages, first, last),
        out_shape=result if last else state,
        in_specs=[SMEM if x.ndim == 1 else VMEM for x in operands],
        out_specs=VMEM if last else (VMEM, VMEM),
        scratch_shapes=[
            pltpu.VMEM((width, width), jnp.float32),
            pltpu.VMEM((width, width), jnp.float32),
            *([pltpu.VMEM((BLK, BLK), jnp.float32), pltpu.VMEM((width, width), jnp.bfloat16)] if last else []),
            pltpu.VMEM((width - BLK, 6 * BLK), jnp.bfloat16),
            pltpu.VMEM((6 * BLK, width - BLK), jnp.bfloat16),
        ],
        compiler_params=pltpu.CompilerParams(vmem_limit_bytes=36 * MIB),
        cost_estimate=pl.CostEstimate(flops=stages * 6_000_000_000, bytes_accessed=4 * MIB, transcendentals=0),
        name="inverse",
    )(*operands)


def score_kernel(halves, bucket_ref, precond_ref, *refs):
    *eval_refs, out_ref = refs
    width = precond_ref.shape[0]
    bucket = bucket_ref[0]
    weight = jnp.zeros(bucket.shape, jnp.float32)
    for level in range(BUCKETS):
        weight = weight + jnp.where(bucket == level, jnp.float32(weight_table[level]), 0.0)
    weight = weight / jnp.sqrt(jnp.float32(width))
    rows = out_ref.shape[0]
    evals = []
    for count in halves:
        some, eval_refs = eval_refs[:count], eval_refs[count:]
        value = some[0][...]
        if count == 2:
            value = jnp.where(pl.program_id(0) < pl.num_programs(0) // 2, value, some[1][...])
        evals.append(value)
    evals = jnp.concatenate(evals, axis=1)
    scores = mm(evals, precond_ref[...])
    for at in range(0, rows, BLK):
        factor = jnp.broadcast_to(weight[:, at : at + BLK], (BLK, BLK)).T
        for to in range(0, out_ref.shape[1], BLK):
            out_ref[at : at + BLK, to : to + BLK] = (
                scores[at : at + BLK, to : to + BLK] * factor
            ).astype(jnp.bfloat16)


def shift(members, stride, by):
    n = lax.axis_size("tr")
    pairs = []
    for i in range(n):
        p = i // stride % members
        pairs.append((i, i + ((p + by) % members - p) * stride))
    return pairs


def scatter_sum(x, members, stride):
    me = lax.axis_index("tr") // stride % members
    chunks = x.reshape(members, -1, BLK)
    mine = lax.dynamic_index_in_dim(chunks, me, keepdims=False)
    got = [
        lax.ppermute(
            lax.dynamic_index_in_dim(chunks, (me + by) % members, keepdims=False), "tr", shift(members, stride, by)
        )
        for by in range(1, members)
    ]
    for piece in got:
        mine = mine + piece
    return mine


def collect(x, members, stride):
    me = lax.axis_index("tr") // stride % members
    got = [x] + [lax.ppermute(x, "tr", shift(members, stride, by)) for by in range(members - 1, 0, -1)]
    if members == 2:
        whole = jnp.where(
            me == 0, jnp.concatenate(got, axis=0), jnp.concatenate(got[::-1], axis=0)
        )
        return whole
    twice = jnp.concatenate(got + got, axis=0)
    return lax.dynamic_slice_in_dim(twice, (members - me) * x.shape[0], members * x.shape[0])


def chip_axes():
    n = lax.axis_size("tr")
    inner = 2 ** ((n.bit_length() - 1) // 2)
    return (inner, 1), (n // inner, inner)


def sum_over_tr(parts):
    axes = chip_axes()
    orders = [axes, axes[::-1]]
    parts = [scatter_sum(x, *order[0]) for x, order in zip(parts, orders)]
    parts = [scatter_sum(x, *order[1]) for x, order in zip(parts, orders)]
    parts = lax.optimization_barrier([collect(x, *order[1]) for x, order in zip(parts, orders)])
    return [collect(x, *order[0]) for x, order in zip(parts, orders)]


def shards(train_grads, eval_grads, eval_bucket, train_valid):
    rows_here, width = train_grads.shape
    total_rows = rows_here * lax.axis_size("tr") * lax.axis_size("ev")
    here = lax.axis_index("ev")
    tr = lax.axis_index("tr")
    swap = [(0, 1), (1, 0)]
    blocks = width // BLK
    half = blocks // 2
    (inner, _), (outer, _) = chip_axes()
    by_ring = eval_grads.shape[1] % BLK == 0

    def across_inner(x):
        return [lax.ppermute(x, "tr", shift(inner, 1, by)) for by in range(1, inner)]

    def along_outer(x):
        return lax.ppermute(x, "tr", shift(outer, inner, 1))

    other_train = lax.ppermute(train_grads, "ev", swap)
    other_valid = lax.ppermute(train_valid, "ev", swap)
    chip_valid = jnp.where(
        here == 0, jnp.concatenate([train_valid, other_valid]), jnp.concatenate([other_valid, train_valid])
    )
    chip_rows = 2 * rows_here
    held = half * (2 * half + 1) // 2 * BLK
    first_held = held // BLK * 13 // 20 * BLK
    *local_gram, turned = pl.pallas_call(
        gram_kernel,
        out_shape=(
            jax.ShapeDtypeStruct((first_held, BLK), jnp.float32),
            jax.ShapeDtypeStruct((held - first_held, BLK), jnp.float32),
            jax.ShapeDtypeStruct((width, chip_rows), jnp.bfloat16),
        ),
        in_specs=[SMEM, VMEM, VMEM, VMEM],
        out_specs=(VMEM,) * 3,
        scratch_shapes=[pltpu.VMEM((chip_rows, width), jnp.bfloat16)],
        compiler_params=pltpu.CompilerParams(vmem_limit_bytes=32 * MIB),
        cost_estimate=pl.CostEstimate(flops=2 * chip_rows * held * BLK, bytes_accessed=6 * MIB, transcendentals=0),
        name="gram",
    )(here.reshape(1), train_grads, other_train, chip_valid[None, :])

    ring = [eval_grads]
    beside = []
    if by_ring:
        ring.append(along_outer(eval_grads))
        beside.append(across_inner(eval_grads))
        local_gram, ring, beside = lax.optimization_barrier((local_gram, ring, beside))

    own_gram = sum_over_tr(local_gram)
    other_gram = [lax.ppermute(x, "ev", swap) for x in own_gram]
    gram = [*own_gram, *other_gram]

    column = (jnp.arange(blocks, dtype=jnp.int32) + half * here) % blocks
    if by_ring:
        gram, ring, beside = lax.optimization_barrier((gram, ring, beside))
        owner = column * BLK // eval_grads.shape[1]
        behind = (tr // inner - owner // inner) % outer
        aside = (tr - owner) % inner
        each = eval_grads.shape[1] // BLK
        place = (behind * inner + aside) * each + column % each
    else:
        gram, eval_grads = lax.optimization_barrier((gram, eval_grads))
        full_eval = lax.all_gather(eval_grads, "tr", axis=1, tiled=True)
        place = column

    def advance():
        if by_ring and len(ring) < outer:
            arrived = ring[-1]
            ring.append(along_outer(arrived))
            beside.append(across_inner(arrived))

    advance()
    state = call_inverse(width, total_rows, 0, 2, (here.reshape(1), *gram), first=True)
    if by_ring:
        state, ring, beside = lax.optimization_barrier((state, ring, beside))
    advance()
    state = call_inverse(width, total_rows, 2, 3, state)
    if by_ring:
        state, ring, beside = lax.optimization_barrier((state, ring, beside))
        while len(ring) < outer:
            advance()
        evals = []
        for arrived, aside in zip(ring, beside):
            evals.append([arrived])
            evals += [[x] for x in aside]
        rows = ring[-1].shape[0] // 2
        for by, before in enumerate(beside[-1], 1):
            top = lax.ppermute(ring[-1][:rows], "tr", shift(inner, 1, by))
            low = along_outer(before[rows:])
            if by == 1:
                evals.append([ring[-1]])
            evals.append([top, low])
    else:
        evals = [[full_eval]]
    precond = call_inverse(width, total_rows, 5, blocks - 5, (place, *state, turned), last=True)

    eval_rows = sum(x.shape[0] for x in evals[0])
    tile = 512
    tiles = eval_rows // tile
    pieces = [x for block in evals for x in block]
    halves = [len(block) for block in evals]
    specs = []
    for block in evals:
        for n, x in enumerate(block):
            each = tiles // len(block)
            specs.append(
                pl.BlockSpec((tile, x.shape[1]), lambda i, low=n * each, each=each: (jnp.clip(i - low, 0, each - 1), 0))
            )
    return pl.pallas_call(
        functools.partial(score_kernel, halves),
        grid=(eval_rows // tile,),
        out_shape=jax.ShapeDtypeStruct((eval_rows, chip_rows), jnp.bfloat16),
        in_specs=[
            pl.BlockSpec((1, 1, tile), lambda i: (i, 0, 0)),
            pl.BlockSpec((width, chip_rows), lambda i: (0, 0)),
            *specs,
        ],
        out_specs=pl.BlockSpec((tile, chip_rows), lambda i: (i, 0)),
        compiler_params=pltpu.CompilerParams(vmem_limit_bytes=24 * MIB),
        cost_estimate=pl.CostEstimate(
            flops=2 * eval_rows * width * chip_rows, bytes_accessed=10 * MIB, transcendentals=0
        ),
        name="scores",
    )(eval_bucket.reshape(eval_rows // tile, 1, tile), precond, *pieces)


def solution(mesh):
    in_specs = (
        P(("grp", "tr", "ev"), None),
        P(("grp", "ev"), "tr"),
        P(("grp", "ev")),
        P(("grp", "tr", "ev")),
    )
    out_specs = P(("grp", "ev"), "tr")
    return jax.shard_map(shards, mesh=mesh, in_specs=in_specs, out_specs=out_specs, check_vma=False)
```

```python
import functools

import jax
import jax.numpy as jnp
from jax import lax
from jax.experimental import pallas as pl
from jax.experimental.pallas import tpu as pltpu
from jax.sharding import PartitionSpec as P

BUCKETS = 8
BLK = 128
MIB = 2**20

damping = 0.1
weight_table = (0.6, 0.9, 1.3, 1.8, 2.4, 3.1, 3.9, 4.8)

VMEM = pl.BlockSpec(memory_space=pltpu.VMEM)
SMEM = pl.BlockSpec(memory_space=pltpu.SMEM)

def split3(x):
    hi = x.astype(jnp.bfloat16)
    rest = x - hi.astype(jnp.float32)
    mid = rest.astype(jnp.bfloat16)
    low = (rest - mid.astype(jnp.float32)).astype(jnp.bfloat16)
    return hi, mid, low


def as_left(x):
    hi, mid, low = split3(x)
    return jnp.concatenate([hi, mid, hi, mid, hi, low], axis=1)


def as_right(x):
    hi, mid, low = split3(x)
    return jnp.concatenate([hi, hi, mid, mid, low, hi], axis=0)


def mm(left, right):
    return jnp.dot(left, right, preferred_element_type=jnp.float32)


def across(x, lane):
    return jnp.broadcast_to(x[:, lane : lane + 1], x.shape)


def down(x, row):
    return jnp.broadcast_to(x[row : row + 1, :], x.shape)


def total(terms):
    while len(terms) > 1:
        terms = [a + b for a, b in zip(terms[::2], terms[1::2])] + terms[len(terms) & ~1 :]
    return terms[0]


def invert_block(block, beside=()):
    lanes = lax.broadcasted_iota(jnp.int32, (8, BLK), 1)
    subs = lax.broadcasted_iota(jnp.int32, (8, BLK), 0)
    count = BLK // 8
    strips = [block[8 * b : 8 * b + 8, :] for b in range(count)]
    group = count // 2
    for m in range(count):
        inside = range(m // group * group, (m // group + 1) * group)
        outside = [b for b in range(count) if b not in inside]
        if m == inside[0]:
            before = as_left(jnp.concatenate([strips[b] for b in outside], axis=0))
        row = strips[m]
        cols = [across(row, 8 * m + t) for t in range(8)]
        for t in range(0, 8, 2):
            first, second = cols[t], cols[t + 1]
            a, b, c = down(first, t), down(second, t), down(second, t + 1)
            scale = 1.0 / (a * c - b * b)
            at_first, at_second = subs == t, subs == t + 1
            own_first, own_second = lanes == 8 * m + t, lanes == 8 * m + t + 1
            upper = jnp.where(own_first, 1.0, jnp.where(own_second, 0.0, down(row, t)))
            lower = jnp.where(own_second, 1.0, jnp.where(own_first, 0.0, down(row, t + 1)))
            lead_first = c * upper - b * lower
            lead_second = a * lower - b * upper
            swept = first * lead_first + second * lead_second
            rest = jnp.where(own_first | own_second, 0.0, row) - swept * scale
            row = jnp.where(at_first, lead_first * scale, jnp.where(at_second, lead_second * scale, rest))
            for s in range(t + 2, 8):
                upper, lower = down(cols[s], t), down(cols[s], t + 1)
                lead_first = c * upper - b * lower
                lead_second = a * lower - b * upper
                swept = first * lead_first + second * lead_second
                cols[s] = jnp.where(
                    at_first,
                    lead_first * scale,
                    jnp.where(at_second, lead_second * scale, cols[s] - swept * scale),
                )
        strips[m] = row
        for piece in beside[m * len(beside) // count : (m + 1) * len(beside) // count]:
            piece()
        done = (lanes >= 8 * m) & (lanes < 8 * m + 8)
        leads = [down(row, t) for t in range(8)]
        for b in [*range(m + 1, inside[-1] + 1), *range(inside[0], m)]:
            old = strips[b]
            strips[b] = jnp.where(done, 0.0, old) - total([across(old, 8 * m + t) * leads[t] for t in range(8)])
        if m == inside[-1]:
            reduced = jnp.concatenate(
                [strips[b] if b in inside else jnp.zeros((8, BLK), jnp.float32) for b in range(count)], axis=0
            )
            swept = mm(before, as_right(reduced))
            done = (lanes >= 8 * inside[0]) & (lanes < 8 * inside[-1] + 8)
            for n, b in enumerate(outside):
                strips[b] = jnp.where(done, 0.0, strips[b]) - swept[8 * n : 8 * n + 8, :]
    return jnp.concatenate(strips, axis=0)


def eliminate(src, dst, held, left_ref, right_ref, last=False):
    size = src.shape[0]
    rest = size - BLK
    pivot = held[...]
    scaled = mm(as_left(pivot), as_right(src[0:BLK, BLK:size]))
    left_ref[...] = as_left(src[BLK:size, 0:BLK])
    right_ref[...] = as_right(scaled)
    dst[rest:size, 0:rest] = scaled
    dst[rest:size, rest:size] = pivot

    def strip(top, tall, at, wide):
        def run():
            dst[top : top + tall, at : at + wide] = src[
                BLK + top : BLK + top + tall, BLK + at : BLK + at + wide
            ] - mm(left_ref[top : top + tall, :], right_ref[:, at : at + wide])

        return run

    def border():
        dst[0:rest, rest:size] = -mm(left_ref[...], as_right(pivot))

    wide = 2 * BLK
    tall = rest if last else rest // 2
    work = [
        strip(top, tall, at, min(wide, rest - at)) for at in range(0, rest, wide) for top in range(0, rest, tall)
    ] + [border]
    if last:
        for piece in work:
            piece()
    else:
        ahead = src[BLK : 2 * BLK, BLK : 2 * BLK] - mm(left_ref[0:BLK, :], right_ref[:, 0:BLK])
        held[...] = invert_block(ahead, work)


def gram_kernel(ev_ref, own_ref, other_ref, valid_ref, *refs):
    parts, turned_ref, chip = refs[:-2], refs[-2], refs[-1]
    here = ev_ref[0]
    rows, width = own_ref.shape
    blocks = width // BLK
    half = blocks // 2
    middle = width // 2
    for order, ref in ((here, own_ref), (1 - here, other_ref)):
        at = pl.ds(pl.multiple_of(order * rows, rows), rows)
        for side in range(2):
            to = pl.ds(pl.multiple_of((here + side) % 2 * middle, middle), middle)
            piece = ref[:, side * middle : (side + 1) * middle]
            chip[at, to] = piece
            turned_ref[to, at] = piece.T
    turned_ref[...] = turned_ref[...] * valid_ref[...].astype(jnp.float32).astype(jnp.bfloat16)
    spots = [(ref, at) for ref in parts for at in range(0, ref.shape[0], BLK)]
    for i in range(half):
        part = mm(
            turned_ref[i * BLK : (i + 1) * BLK, :],
            chip[:, i * BLK : (i + half) * BLK],
        )
        for j in range(half):
            ref, at = spots[i * half + j]
            ref[at : at + BLK, :] = part[:, j * BLK : (j + 1) * BLK]
    for t in range(half // 2):
        i = here * (half // 2) + t
        ref, at = spots[half * half + t]
        ref[at : at + BLK, :] = mm(
            turned_ref[pl.ds(pl.multiple_of(i * BLK, BLK), BLK), :],
            chip[:, pl.ds(pl.multiple_of((i + half) * BLK, BLK), BLK)],
        )


def inverse_kernel(total_rows, stages, first, last, *refs):
    if first:
        ev_ref, *parts, matrix_out, held_out, one, two, left_ref, right_ref = refs
    elif last:
        place_ref, matrix_in, held_in, turned_ref, out_ref, one, two, held_out, placed, left_ref, right_ref = refs
    else:
        matrix_in, held_in, matrix_out, held_out, one, two, left_ref, right_ref = refs
    size = one.shape[0]
    blocks = size // BLK
    half = blocks // 2
    if first:
        spots = [(ref, at) for ref in parts for at in range(0, ref.shape[0], BLK)]
        rows = lax.broadcasted_iota(jnp.int32, (BLK, BLK), 0)
        cols = lax.broadcasted_iota(jnp.int32, (BLK, BLK), 1)
        ridge = jnp.where(rows == cols, jnp.float32(damping), 0.0)
        count = len(spots) // 2
        for i in range(blocks):
            for j in range(half):
                ref, at = spots[i // half * count + i % half * half + j]
                c = (i + j) % blocks
                value = ref[at : at + BLK, :] / total_rows
                if j == 0:
                    value = value + ridge
                one[i * BLK : (i + 1) * BLK, c * BLK : (c + 1) * BLK] = value
                if j > 0:
                    one[c * BLK : (c + 1) * BLK, i * BLK : (i + 1) * BLK] = value.T
        for side in range(2):
            for t in range(half // 2):
                ref, at = spots[side * count + half * half + t]
                i = (ev_ref[0] + side) % 2 * (half // 2) + t
                value = ref[at : at + BLK, :] / total_rows
                upper = pl.ds(pl.multiple_of(i * BLK, BLK), BLK)
                lower = pl.ds(pl.multiple_of((i + half) * BLK, BLK), BLK)
                one[upper, lower] = value.T if side else value
                one[lower, upper] = value if side else value.T
        held_out[...] = invert_block(one[0:BLK, 0:BLK])
        now = one
    else:
        held_out[...] = held_in[...]
        now = matrix_in
    for stage in range(stages):
        if stage == stages - 1 and not last:
            then = matrix_out
        else:
            then = one if now is two else two
        eliminate(now, then, held_out, left_ref, right_ref, last=last and stage == stages - 1)
        now = then
    if last:
        for i in range(blocks):
            to = pl.ds(pl.multiple_of(place_ref[i] * BLK, BLK), BLK)
            placed[to, :] = now[i * BLK : (i + 1) * BLK, :].astype(jnp.bfloat16)
        wide = 2 * BLK
        for at in range(0, out_ref.shape[1], wide):
            out_ref[:, at : at + wide] = mm(placed[...], turned_ref[:, at : at + wide]).astype(jnp.bfloat16)


def call_inverse(width, total_rows, stages, operands, first=False, last=False):
    state = (
        jax.ShapeDtypeStruct((width, width), jnp.float32),
        jax.ShapeDtypeStruct((BLK, BLK), jnp.float32),
    )
    result = jax.ShapeDtypeStruct((width, operands[-1].shape[-1]), jnp.bfloat16)
    return pl.pallas_call(
        functools.partial(inverse_kernel, total_rows, stages, first, last),
        out_shape=result if last else state,
        in_specs=[SMEM if x.ndim == 1 else VMEM for x in operands],
        out_specs=VMEM if last else (VMEM, VMEM),
        scratch_shapes=[
            pltpu.VMEM((width, width), jnp.float32),
            pltpu.VMEM((width, width), jnp.float32),
            *([pltpu.VMEM((BLK, BLK), jnp.float32), pltpu.VMEM((width, width), jnp.bfloat16)] if last else []),
            pltpu.VMEM((width - BLK, 6 * BLK), jnp.bfloat16),
            pltpu.VMEM((6 * BLK, width - BLK), jnp.bfloat16),
        ],
        compiler_params=pltpu.CompilerParams(vmem_limit_bytes=36 * MIB),
        cost_estimate=pl.CostEstimate(flops=stages * 6_000_000_000, bytes_accessed=4 * MIB, transcendentals=0),
        name="inverse",
    )(*operands)


def score_kernel(halves, bucket_ref, precond_ref, *refs):
    *eval_refs, out_ref = refs
    width = precond_ref.shape[0]
    bucket = bucket_ref[0]
    weight = jnp.zeros(bucket.shape, jnp.float32)
    for level in range(BUCKETS):
        weight = weight + jnp.where(bucket == level, jnp.float32(weight_table[level]), 0.0)
    weight = weight / jnp.sqrt(jnp.float32(width))
    rows = out_ref.shape[0]
    evals = []
    for count in halves:
        some, eval_refs = eval_refs[:count], eval_refs[count:]
        value = some[0][...]
        if count == 2:
            value = jnp.where(pl.program_id(0) < pl.num_programs(0) // 2, value, some[1][...])
        evals.append(value)
    evals = jnp.concatenate(evals, axis=1)
    scores = mm(evals, precond_ref[...])
    for at in range(0, rows, BLK):
        factor = jnp.broadcast_to(weight[:, at : at + BLK], (BLK, BLK)).T
        for to in range(0, out_ref.shape[1], BLK):
            out_ref[at : at + BLK, to : to + BLK] = (
                scores[at : at + BLK, to : to + BLK] * factor
            ).astype(jnp.bfloat16)


def shift(members, stride, by):
    n = lax.axis_size("tr")
    pairs = []
    for i in range(n):
        p = i // stride % members
        pairs.append((i, i + ((p + by) % members - p) * stride))
    return pairs


def scatter_sum(x, members, stride):
    me = lax.axis_index("tr") // stride % members
    chunks = x.reshape(members, -1, BLK)
    mine = lax.dynamic_index_in_dim(chunks, me, keepdims=False)
    got = [
        lax.ppermute(
            lax.dynamic_index_in_dim(chunks, (me + by) % members, keepdims=False), "tr", shift(members, stride, by)
        )
        for by in range(1, members)
    ]
    for piece in got:
        mine = mine + piece
    return mine


def collect(x, members, stride):
    me = lax.axis_index("tr") // stride % members
    got = [x] + [lax.ppermute(x, "tr", shift(members, stride, by)) for by in range(members - 1, 0, -1)]
    if members == 2:
        whole = jnp.where(
            me == 0, jnp.concatenate(got, axis=0), jnp.concatenate(got[::-1], axis=0)
        )
        return whole
    twice = jnp.concatenate(got + got, axis=0)
    return lax.dynamic_slice_in_dim(twice, (members - me) * x.shape[0], members * x.shape[0])


def chip_axes():
    n = lax.axis_size("tr")
    inner = 2 ** ((n.bit_length() - 1) // 2)
    return (inner, 1), (n // inner, inner)


def sum_over_tr(parts):
    axes = chip_axes()
    orders = [axes, axes[::-1]]
    parts = [scatter_sum(x, *order[0]) for x, order in zip(parts, orders)]
    parts = [scatter_sum(x, *order[1]) for x, order in zip(parts, orders)]
    parts = lax.optimization_barrier([collect(x, *order[1]) for x, order in zip(parts, orders)])
    return [collect(x, *order[0]) for x, order in zip(parts, orders)]


def shards(train_grads, eval_grads, eval_bucket, train_valid):
    rows_here, width = train_grads.shape
    total_rows = rows_here * lax.axis_size("tr") * lax.axis_size("ev")
    here = lax.axis_index("ev")
    tr = lax.axis_index("tr")
    swap = [(0, 1), (1, 0)]
    blocks = width // BLK
    half = blocks // 2
    (inner, _), (outer, _) = chip_axes()
    by_ring = eval_grads.shape[1] % BLK == 0

    def across_inner(x):
        return [lax.ppermute(x, "tr", shift(inner, 1, by)) for by in range(1, inner)]

    def along_outer(x):
        return lax.ppermute(x, "tr", shift(outer, inner, 1))

    other_train = lax.ppermute(train_grads, "ev", swap)
    other_valid = lax.ppermute(train_valid, "ev", swap)
    chip_valid = jnp.where(
        here == 0, jnp.concatenate([train_valid, other_valid]), jnp.concatenate([other_valid, train_valid])
    )
    chip_rows = 2 * rows_here
    held = half * (2 * half + 1) // 2 * BLK
    first_held = held // BLK * 13 // 20 * BLK
    *local_gram, turned = pl.pallas_call(
        gram_kernel,
        out_shape=(
            jax.ShapeDtypeStruct((first_held, BLK), jnp.float32),
            jax.ShapeDtypeStruct((held - first_held, BLK), jnp.float32),
            jax.ShapeDtypeStruct((width, chip_rows), jnp.bfloat16),
        ),
        in_specs=[SMEM, VMEM, VMEM, VMEM],
        out_specs=(VMEM,) * 3,
        scratch_shapes=[pltpu.VMEM((chip_rows, width), jnp.bfloat16)],
        compiler_params=pltpu.CompilerParams(vmem_limit_bytes=32 * MIB),
        cost_estimate=pl.CostEstimate(flops=2 * chip_rows * held * BLK, bytes_accessed=6 * MIB, transcendentals=0),
        name="gram",
    )(here.reshape(1), train_grads, other_train, chip_valid[None, :])

    ring = [eval_grads]
    beside = []
    if by_ring:
        ring.append(along_outer(eval_grads))
        beside.append(across_inner(eval_grads))
        local_gram, ring, beside = lax.optimization_barrier((local_gram, ring, beside))

    own_gram = sum_over_tr(local_gram)
    other_gram = [lax.ppermute(x, "ev", swap) for x in own_gram]
    gram = [*own_gram, *other_gram]

    column = (jnp.arange(blocks, dtype=jnp.int32) + half * here) % blocks
    if by_ring:
        gram, ring, beside = lax.optimization_barrier((gram, ring, beside))
        owner = column * BLK // eval_grads.shape[1]
        behind = (tr // inner - owner // inner) % outer
        aside = (tr - owner) % inner
        each = eval_grads.shape[1] // BLK
        place = (behind * inner + aside) * each + column % each
    else:
        gram, eval_grads = lax.optimization_barrier((gram, eval_grads))
        full_eval = lax.all_gather(eval_grads, "tr", axis=1, tiled=True)
        place = column

    def advance():
        if by_ring and len(ring) < outer:
            arrived = ring[-1]
            ring.append(along_outer(arrived))
            beside.append(across_inner(arrived))

    advance()
    state = call_inverse(width, total_rows, 2, (here.reshape(1), *gram), first=True)
    if by_ring:
        state, ring, beside = lax.optimization_barrier((state, ring, beside))
    advance()
    state = call_inverse(width, total_rows, 3, state)
    if by_ring:
        state, ring, beside = lax.optimization_barrier((state, ring, beside))
        while len(ring) < outer:
            advance()
        evals = []
        for arrived, aside in zip(ring, beside):
            evals.append([arrived])
            evals += [[x] for x in aside]
        rows = ring[-1].shape[0] // 2
        for by, before in enumerate(beside[-1], 1):
            top = lax.ppermute(ring[-1][:rows], "tr", shift(inner, 1, by))
            low = along_outer(before[rows:])
            if by == 1:
                evals.append([ring[-1]])
            evals.append([top, low])
    else:
        evals = [[full_eval]]
    precond = call_inverse(width, total_rows, blocks - 5, (place, *state, turned), last=True)

    eval_rows = sum(x.shape[0] for x in evals[0])
    tile = 512
    tiles = eval_rows // tile
    pieces = [x for block in evals for x in block]
    halves = [len(block) for block in evals]
    specs = []
    for block in evals:
        for n, x in enumerate(block):
            each = tiles // len(block)
            specs.append(
                pl.BlockSpec((tile, x.shape[1]), lambda i, low=n * each, each=each: (jnp.clip(i - low, 0, each - 1), 0))
            )
    return pl.pallas_call(
        functools.partial(score_kernel, halves),
        grid=(eval_rows // tile,),
        out_shape=jax.ShapeDtypeStruct((eval_rows, chip_rows), jnp.bfloat16),
        in_specs=[
            pl.BlockSpec((1, 1, tile), lambda i: (i, 0, 0)),
            pl.BlockSpec((width, chip_rows), lambda i: (0, 0)),
            *specs,
        ],
        out_specs=pl.BlockSpec((tile, chip_rows), lambda i: (i, 0)),
        compiler_params=pltpu.CompilerParams(vmem_limit_bytes=24 * MIB),
        cost_estimate=pl.CostEstimate(
            flops=2 * eval_rows * width * chip_rows, bytes_accessed=10 * MIB, transcendentals=0
        ),
        name="scores",
    )(eval_bucket.reshape(eval_rows // tile, 1, tile), precond, *pieces)


def solution(mesh):
    in_specs = (
        P(("grp", "tr", "ev"), None),
        P(("grp", "ev"), "tr"),
        P(("grp", "ev")),
        P(("grp", "tr", "ev")),
    )
    out_specs = P(("grp", "ev"), "tr")
    return jax.shard_map(shards, mesh=mesh, in_specs=in_specs, out_specs=out_specs, check_vma=False)
```

```python
import functools

import jax
import jax.numpy as jnp
from jax import lax
from jax.experimental import pallas as pl
from jax.experimental.pallas import tpu as pltpu
from jax.sharding import PartitionSpec as P

BUCKETS = 8
BLK = 128
MIB = 2**20

damping = 0.1
weight_table = (0.6, 0.9, 1.3, 1.8, 2.4, 3.1, 3.9, 4.8)

VMEM = pl.BlockSpec(memory_space=pltpu.VMEM)
SMEM = pl.BlockSpec(memory_space=pltpu.SMEM)

def split3(x):
    hi = x.astype(jnp.bfloat16)
    rest = x - hi.astype(jnp.float32)
    mid = rest.astype(jnp.bfloat16)
    low = (rest - mid.astype(jnp.float32)).astype(jnp.bfloat16)
    return hi, mid, low


def as_left(x):
    hi, mid, low = split3(x)
    return jnp.concatenate([hi, mid, hi, mid, hi, low], axis=1)


def as_right(x):
    hi, mid, low = split3(x)
    return jnp.concatenate([hi, hi, mid, mid, low, hi], axis=0)


def mm(left, right):
    return jnp.dot(left, right, preferred_element_type=jnp.float32)


def across(x, lane):
    return jnp.broadcast_to(x[:, lane : lane + 1], x.shape)


def down(x, row):
    return jnp.broadcast_to(x[row : row + 1, :], x.shape)


def total(terms):
    while len(terms) > 1:
        terms = [a + b for a, b in zip(terms[::2], terms[1::2])] + terms[len(terms) & ~1 :]
    return terms[0]


def inverse_of(x):
    guess = pltpu.reciprocal(x, approx=True)
    guess = guess * (2.0 - x * guess)
    return guess * (2.0 - x * guess)


def invert_block(block, beside=()):
    lanes = lax.broadcasted_iota(jnp.int32, (8, BLK), 1)
    subs = lax.broadcasted_iota(jnp.int32, (8, BLK), 0)
    count = BLK // 8
    strips = [block[8 * b : 8 * b + 8, :] for b in range(count)]
    group = count // 2
    for m in range(count):
        inside = range(m // group * group, (m // group + 1) * group)
        outside = [b for b in range(count) if b not in inside]
        if m == inside[0]:
            before = as_left(jnp.concatenate([strips[b] for b in outside], axis=0))
        row = strips[m]
        cols = [across(row, 8 * m + t) for t in range(8)]
        for t in range(0, 8, 2):
            first, second = cols[t], cols[t + 1]
            a, b, c = down(first, t), down(second, t), down(second, t + 1)
            scale = inverse_of(a * c - b * b)
            at_first, at_second = subs == t, subs == t + 1
            own_first, own_second = lanes == 8 * m + t, lanes == 8 * m + t + 1
            upper = jnp.where(own_first, 1.0, jnp.where(own_second, 0.0, down(row, t)))
            lower = jnp.where(own_second, 1.0, jnp.where(own_first, 0.0, down(row, t + 1)))
            lead_first = c * upper - b * lower
            lead_second = a * lower - b * upper
            swept = first * lead_first + second * lead_second
            rest = jnp.where(own_first | own_second, 0.0, row) - swept * scale
            row = jnp.where(at_first, lead_first * scale, jnp.where(at_second, lead_second * scale, rest))
            for s in range(t + 2, 8):
                upper, lower = down(cols[s], t), down(cols[s], t + 1)
                lead_first = c * upper - b * lower
                lead_second = a * lower - b * upper
                swept = first * lead_first + second * lead_second
                cols[s] = jnp.where(
                    at_first,
                    lead_first * scale,
                    jnp.where(at_second, lead_second * scale, cols[s] - swept * scale),
                )
        strips[m] = row
        for piece in beside[m * len(beside) // count : (m + 1) * len(beside) // count]:
            piece()
        done = (lanes >= 8 * m) & (lanes < 8 * m + 8)
        leads = [down(row, t) for t in range(8)]
        for b in [*range(m + 1, inside[-1] + 1), *range(inside[0], m)]:
            old = strips[b]
            strips[b] = jnp.where(done, 0.0, old) - total([across(old, 8 * m + t) * leads[t] for t in range(8)])
        if m == inside[-1]:
            reduced = jnp.concatenate(
                [strips[b] if b in inside else jnp.zeros((8, BLK), jnp.float32) for b in range(count)], axis=0
            )
            swept = mm(before, as_right(reduced))
            done = (lanes >= 8 * inside[0]) & (lanes < 8 * inside[-1] + 8)
            for n, b in enumerate(outside):
                strips[b] = jnp.where(done, 0.0, strips[b]) - swept[8 * n : 8 * n + 8, :]
    return jnp.concatenate(strips, axis=0)


def eliminate(src, dst, held, left_ref, right_ref, last=False):
    size = src.shape[0]
    rest = size - BLK
    pivot = held[...]
    pivot_parts = as_left(pivot)
    scaled = mm(pivot_parts, as_right(src[0:BLK, BLK : 2 * BLK]))
    ahead_parts = as_right(scaled)
    if not last:
        ahead = src[BLK : 2 * BLK, BLK : 2 * BLK] - mm(as_left(src[BLK : 2 * BLK, 0:BLK]), ahead_parts)
    right_ref[:, 0:BLK] = ahead_parts
    dst[rest:size, 0:BLK] = scaled
    dst[rest:size, rest:size] = pivot

    def fill_right():
        others = mm(pivot_parts, as_right(src[0:BLK, 2 * BLK : size]))
        right_ref[:, BLK:rest] = as_right(others)
        dst[rest:size, BLK:rest] = others

    def fill_left():
        left_ref[...] = as_left(src[BLK:size, 0:BLK])

    def strip(top, tall, at, wide):
        def run():
            dst[top : top + tall, at : at + wide] = src[
                BLK + top : BLK + top + tall, BLK + at : BLK + at + wide
            ] - mm(left_ref[top : top + tall, :], right_ref[:, at : at + wide])

        return run

    def border():
        dst[0:rest, rest:size] = -mm(left_ref[...], as_right(pivot))

    wide = 2 * BLK
    tall = rest if last else rest // 2
    work = [fill_left, fill_right] + [
        strip(top, tall, at, min(wide, rest - at)) for at in range(0, rest, wide) for top in range(0, rest, tall)
    ] + [border]
    if last:
        for piece in work:
            piece()
    else:
        held[...] = invert_block(ahead, work)


def gram_kernel(ev_ref, own_ref, other_ref, valid_ref, *refs):
    parts, turned_ref, chip = refs[:-2], refs[-2], refs[-1]
    here = ev_ref[0]
    rows, width = own_ref.shape
    blocks = width // BLK
    half = blocks // 2
    middle = width // 2
    for order, ref in ((here, own_ref), (1 - here, other_ref)):
        at = pl.ds(pl.multiple_of(order * rows, rows), rows)
        for side in range(2):
            to = pl.ds(pl.multiple_of((here + side) % 2 * middle, middle), middle)
            piece = ref[:, side * middle : (side + 1) * middle]
            chip[at, to] = piece
            turned_ref[to, at] = piece.T
    turned_ref[...] = turned_ref[...] * valid_ref[...].astype(jnp.float32).astype(jnp.bfloat16)
    spots = [(ref, at) for ref in parts for at in range(0, ref.shape[0], BLK)]
    for i in range(half):
        part = mm(
            turned_ref[i * BLK : (i + 1) * BLK, :],
            chip[:, i * BLK : (i + half) * BLK],
        )
        for j in range(half):
            ref, at = spots[i * half + j]
            ref[at : at + BLK, :] = part[:, j * BLK : (j + 1) * BLK]
    for t in range(half // 2):
        i = here * (half // 2) + t
        ref, at = spots[half * half + t]
        ref[at : at + BLK, :] = mm(
            turned_ref[pl.ds(pl.multiple_of(i * BLK, BLK), BLK), :],
            chip[:, pl.ds(pl.multiple_of((i + half) * BLK, BLK), BLK)],
        )


def inverse_kernel(total_rows, stages, first, last, *refs):
    if first:
        ev_ref, *parts, matrix_out, held_out, one, two, left_ref, right_ref = refs
    elif last:
        place_ref, matrix_in, held_in, turned_ref, out_ref, one, two, held_out, placed, left_ref, right_ref = refs
    else:
        matrix_in, held_in, matrix_out, held_out, one, two, left_ref, right_ref = refs
    size = one.shape[0]
    blocks = size // BLK
    half = blocks // 2
    if first:
        spots = [(ref, at) for ref in parts for at in range(0, ref.shape[0], BLK)]
        rows = lax.broadcasted_iota(jnp.int32, (BLK, BLK), 0)
        cols = lax.broadcasted_iota(jnp.int32, (BLK, BLK), 1)
        ridge = jnp.where(rows == cols, jnp.float32(damping), 0.0)
        count = len(spots) // 2
        for i in range(blocks):
            for j in range(half):
                ref, at = spots[i // half * count + i % half * half + j]
                c = (i + j) % blocks
                value = ref[at : at + BLK, :] / total_rows
                if j == 0:
                    value = value + ridge
                one[i * BLK : (i + 1) * BLK, c * BLK : (c + 1) * BLK] = value
                if j > 0:
                    one[c * BLK : (c + 1) * BLK, i * BLK : (i + 1) * BLK] = value.T
        for side in range(2):
            for t in range(half // 2):
                ref, at = spots[side * count + half * half + t]
                i = (ev_ref[0] + side) % 2 * (half // 2) + t
                value = ref[at : at + BLK, :] / total_rows
                upper = pl.ds(pl.multiple_of(i * BLK, BLK), BLK)
                lower = pl.ds(pl.multiple_of((i + half) * BLK, BLK), BLK)
                one[upper, lower] = value.T if side else value
                one[lower, upper] = value if side else value.T
        held_out[...] = invert_block(one[0:BLK, 0:BLK])
        now = one
    else:
        held_out[...] = held_in[...]
        now = matrix_in
    for stage in range(stages):
        if stage == stages - 1 and not last:
            then = matrix_out
        else:
            then = one if now is two else two
        eliminate(now, then, held_out, left_ref, right_ref, last=last and stage == stages - 1)
        now = then
    if last:
        for i in range(blocks):
            to = pl.ds(pl.multiple_of(place_ref[i] * BLK, BLK), BLK)
            placed[to, :] = now[i * BLK : (i + 1) * BLK, :].astype(jnp.bfloat16)
        wide = 2 * BLK
        for at in range(0, out_ref.shape[1], wide):
            out_ref[:, at : at + wide] = mm(placed[...], turned_ref[:, at : at + wide]).astype(jnp.bfloat16)


def call_inverse(width, total_rows, stages, operands, first=False, last=False):
    state = (
        jax.ShapeDtypeStruct((width, width), jnp.float32),
        jax.ShapeDtypeStruct((BLK, BLK), jnp.float32),
    )
    result = jax.ShapeDtypeStruct((width, operands[-1].shape[-1]), jnp.bfloat16)
    return pl.pallas_call(
        functools.partial(inverse_kernel, total_rows, stages, first, last),
        out_shape=result if last else state,
        in_specs=[SMEM if x.ndim == 1 else VMEM for x in operands],
        out_specs=VMEM if last else (VMEM, VMEM),
        scratch_shapes=[
            pltpu.VMEM((width, width), jnp.float32),
            pltpu.VMEM((width, width), jnp.float32),
            *([pltpu.VMEM((BLK, BLK), jnp.float32), pltpu.VMEM((width, width), jnp.bfloat16)] if last else []),
            pltpu.VMEM((width - BLK, 6 * BLK), jnp.bfloat16),
            pltpu.VMEM((6 * BLK, width - BLK), jnp.bfloat16),
        ],
        compiler_params=pltpu.CompilerParams(vmem_limit_bytes=36 * MIB),
        cost_estimate=pl.CostEstimate(flops=stages * 6_000_000_000, bytes_accessed=4 * MIB, transcendentals=0),
        name="inverse",
    )(*operands)


def score_kernel(halves, bucket_ref, precond_ref, *refs):
    *eval_refs, out_ref = refs
    width = precond_ref.shape[0]
    bucket = bucket_ref[0]
    weight = jnp.zeros(bucket.shape, jnp.float32)
    for level in range(BUCKETS):
        weight = weight + jnp.where(bucket == level, jnp.float32(weight_table[level]), 0.0)
    weight = weight / jnp.sqrt(jnp.float32(width))
    rows = out_ref.shape[0]
    evals = []
    for count in halves:
        some, eval_refs = eval_refs[:count], eval_refs[count:]
        value = some[0][...]
        if count == 2:
            value = jnp.where(pl.program_id(0) < pl.num_programs(0) // 2, value, some[1][...])
        evals.append(value)
    evals = jnp.concatenate(evals, axis=1)
    scores = mm(evals, precond_ref[...])
    for at in range(0, rows, BLK):
        factor = jnp.broadcast_to(weight[:, at : at + BLK], (BLK, BLK)).T
        for to in range(0, out_ref.shape[1], BLK):
            out_ref[at : at + BLK, to : to + BLK] = (
                scores[at : at + BLK, to : to + BLK] * factor
            ).astype(jnp.bfloat16)


def shift(members, stride, by):
    n = lax.axis_size("tr")
    pairs = []
    for i in range(n):
        p = i // stride % members
        pairs.append((i, i + ((p + by) % members - p) * stride))
    return pairs


def scatter_sum(x, members, stride):
    me = lax.axis_index("tr") // stride % members
    chunks = x.reshape(members, -1, BLK)
    mine = lax.dynamic_index_in_dim(chunks, me, keepdims=False)
    got = [
        lax.ppermute(
            lax.dynamic_index_in_dim(chunks, (me + by) % members, keepdims=False), "tr", shift(members, stride, by)
        )
        for by in range(1, members)
    ]
    for piece in got:
        mine = mine + piece
    return mine


def collect(x, members, stride):
    me = lax.axis_index("tr") // stride % members
    got = [x] + [lax.ppermute(x, "tr", shift(members, stride, by)) for by in range(members - 1, 0, -1)]
    if members == 2:
        whole = jnp.where(
            me == 0, jnp.concatenate(got, axis=0), jnp.concatenate(got[::-1], axis=0)
        )
        return whole
    twice = jnp.concatenate(got + got, axis=0)
    return lax.dynamic_slice_in_dim(twice, (members - me) * x.shape[0], members * x.shape[0])


def chip_axes():
    n = lax.axis_size("tr")
    inner = 2 ** ((n.bit_length() - 1) // 2)
    return (inner, 1), (n // inner, inner)


def sum_over_tr(parts):
    axes = chip_axes()
    orders = [axes, axes[::-1]]
    parts = [scatter_sum(x, *order[0]) for x, order in zip(parts, orders)]
    parts = [scatter_sum(x, *order[1]) for x, order in zip(parts, orders)]
    parts = lax.optimization_barrier([collect(x, *order[1]) for x, order in zip(parts, orders)])
    return [collect(x, *order[0]) for x, order in zip(parts, orders)]


def shards(train_grads, eval_grads, eval_bucket, train_valid):
    rows_here, width = train_grads.shape
    total_rows = rows_here * lax.axis_size("tr") * lax.axis_size("ev")
    here = lax.axis_index("ev")
    tr = lax.axis_index("tr")
    swap = [(0, 1), (1, 0)]
    blocks = width // BLK
    half = blocks // 2
    (inner, _), (outer, _) = chip_axes()
    by_ring = eval_grads.shape[1] % BLK == 0

    def across_inner(x):
        return [lax.ppermute(x, "tr", shift(inner, 1, by)) for by in range(1, inner)]

    def along_outer(x):
        return lax.ppermute(x, "tr", shift(outer, inner, 1))

    other_train = lax.ppermute(train_grads, "ev", swap)
    other_valid = lax.ppermute(train_valid, "ev", swap)
    chip_valid = jnp.where(
        here == 0, jnp.concatenate([train_valid, other_valid]), jnp.concatenate([other_valid, train_valid])
    )
    chip_rows = 2 * rows_here
    held = half * (2 * half + 1) // 2 * BLK
    first_held = held // BLK * 13 // 20 * BLK
    *local_gram, turned = pl.pallas_call(
        gram_kernel,
        out_shape=(
            jax.ShapeDtypeStruct((first_held, BLK), jnp.float32),
            jax.ShapeDtypeStruct((held - first_held, BLK), jnp.float32),
            jax.ShapeDtypeStruct((width, chip_rows), jnp.bfloat16),
        ),
        in_specs=[SMEM, VMEM, VMEM, VMEM],
        out_specs=(VMEM,) * 3,
        scratch_shapes=[pltpu.VMEM((chip_rows, width), jnp.bfloat16)],
        compiler_params=pltpu.CompilerParams(vmem_limit_bytes=32 * MIB),
        cost_estimate=pl.CostEstimate(flops=2 * chip_rows * held * BLK, bytes_accessed=6 * MIB, transcendentals=0),
        name="gram",
    )(here.reshape(1), train_grads, other_train, chip_valid[None, :])

    ring = [eval_grads]
    beside = []
    if by_ring:
        ring.append(along_outer(eval_grads))
        beside.append(across_inner(eval_grads))
        local_gram, ring, beside = lax.optimization_barrier((local_gram, ring, beside))

    own_gram = sum_over_tr(local_gram)
    other_gram = [lax.ppermute(x, "ev", swap) for x in own_gram]
    gram = [*own_gram, *other_gram]

    column = (jnp.arange(blocks, dtype=jnp.int32) + half * here) % blocks
    if by_ring:
        gram, ring, beside = lax.optimization_barrier((gram, ring, beside))
        owner = column * BLK // eval_grads.shape[1]
        behind = (tr // inner - owner // inner) % outer
        aside = (tr - owner) % inner
        each = eval_grads.shape[1] // BLK
        place = (behind * inner + aside) * each + column % each
    else:
        gram, eval_grads = lax.optimization_barrier((gram, eval_grads))
        full_eval = lax.all_gather(eval_grads, "tr", axis=1, tiled=True)
        place = column

    def advance():
        if by_ring and len(ring) < outer:
            arrived = ring[-1]
            ring.append(along_outer(arrived))
            beside.append(across_inner(arrived))

    advance()
    state = call_inverse(width, total_rows, 2, (here.reshape(1), *gram), first=True)
    if by_ring:
        state, ring, beside = lax.optimization_barrier((state, ring, beside))
    advance()
    state = call_inverse(width, total_rows, 3, state)
    if by_ring:
        state, ring, beside = lax.optimization_barrier((state, ring, beside))
        while len(ring) < outer:
            advance()
        evals = []
        for arrived, aside in zip(ring, beside):
            evals.append([arrived])
            evals += [[x] for x in aside]
        rows = ring[-1].shape[0] // 2
        for by, before in enumerate(beside[-1], 1):
            top = lax.ppermute(ring[-1][:rows], "tr", shift(inner, 1, by))
            low = along_outer(before[rows:])
            if by == 1:
                evals.append([ring[-1]])
            evals.append([top, low])
    else:
        evals = [[full_eval]]
    precond = call_inverse(width, total_rows, blocks - 5, (place, *state, turned), last=True)

    eval_rows = sum(x.shape[0] for x in evals[0])
    tile = 512
    tiles = eval_rows // tile
    pieces = [x for block in evals for x in block]
    halves = [len(block) for block in evals]
    specs = []
    for block in evals:
        for n, x in enumerate(block):
            each = tiles // len(block)
            specs.append(
                pl.BlockSpec((tile, x.shape[1]), lambda i, low=n * each, each=each: (jnp.clip(i - low, 0, each - 1), 0))
            )
    return pl.pallas_call(
        functools.partial(score_kernel, halves),
        grid=(eval_rows // tile,),
        out_shape=jax.ShapeDtypeStruct((eval_rows, chip_rows), jnp.bfloat16),
        in_specs=[
            pl.BlockSpec((1, 1, tile), lambda i: (i, 0, 0)),
            pl.BlockSpec((width, chip_rows), lambda i: (0, 0)),
            *specs,
        ],
        out_specs=pl.BlockSpec((tile, chip_rows), lambda i: (i, 0)),
        compiler_params=pltpu.CompilerParams(vmem_limit_bytes=24 * MIB),
        cost_estimate=pl.CostEstimate(
            flops=2 * eval_rows * width * chip_rows, bytes_accessed=10 * MIB, transcendentals=0
        ),
        name="scores",
    )(eval_bucket.reshape(eval_rows // tile, 1, tile), precond, *pieces)


def solution(mesh):
    in_specs = (
        P(("grp", "tr", "ev"), None),
        P(("grp", "ev"), "tr"),
        P(("grp", "ev")),
        P(("grp", "tr", "ev")),
    )
    out_specs = P(("grp", "ev"), "tr")
    return jax.shard_map(shards, mesh=mesh, in_specs=in_specs, out_specs=out_specs, check_vma=False)
```

```python
import functools

import jax
import jax.numpy as jnp
from jax import lax
from jax.experimental import pallas as pl
from jax.experimental.pallas import tpu as pltpu
from jax.sharding import PartitionSpec as P

BUCKETS = 8
BLK = 128
MIB = 2**20

damping = 0.1
weight_table = (0.6, 0.9, 1.3, 1.8, 2.4, 3.1, 3.9, 4.8)

VMEM = pl.BlockSpec(memory_space=pltpu.VMEM)
SMEM = pl.BlockSpec(memory_space=pltpu.SMEM)

def split3(x):
    hi = x.astype(jnp.bfloat16)
    rest = x - hi.astype(jnp.float32)
    mid = rest.astype(jnp.bfloat16)
    low = (rest - mid.astype(jnp.float32)).astype(jnp.bfloat16)
    return hi, mid, low


def as_left(x):
    hi, mid, low = split3(x)
    return jnp.concatenate([hi, mid, hi, mid, hi, low], axis=1)


def as_right(x):
    hi, mid, low = split3(x)
    return jnp.concatenate([hi, hi, mid, mid, low, hi], axis=0)


def mm(left, right):
    return jnp.dot(left, right, preferred_element_type=jnp.float32)


def across(x, lane):
    return jnp.broadcast_to(x[:, lane : lane + 1], x.shape)


def down(x, row):
    return jnp.broadcast_to(x[row : row + 1, :], x.shape)


def total(terms):
    while len(terms) > 1:
        terms = [a + b for a, b in zip(terms[::2], terms[1::2])] + terms[len(terms) & ~1 :]
    return terms[0]


def inverse_of(x):
    guess = pltpu.reciprocal(x, approx=True)
    guess = guess * (2.0 - x * guess)
    return guess * (2.0 - x * guess)


def invert_block(block, beside=()):
    lanes = lax.broadcasted_iota(jnp.int32, (8, BLK), 1)
    subs = lax.broadcasted_iota(jnp.int32, (8, BLK), 0)
    count = BLK // 8
    strips = [block[8 * b : 8 * b + 8, :] for b in range(count)]
    group = count // 2
    for m in range(count):
        inside = range(m // group * group, (m // group + 1) * group)
        outside = [b for b in range(count) if b not in inside]
        if m == inside[0]:
            before = as_left(jnp.concatenate([strips[b] for b in outside], axis=0))
        row = strips[m]
        cols = [across(row, 8 * m + t) for t in range(8)]
        for t in range(0, 8, 2):
            first, second = cols[t], cols[t + 1]
            a, b, c = down(first, t), down(second, t), down(second, t + 1)
            scale = inverse_of(a * c - b * b)
            at_first, at_second = subs == t, subs == t + 1
            own_first, own_second = lanes == 8 * m + t, lanes == 8 * m + t + 1
            upper = jnp.where(own_first, 1.0, jnp.where(own_second, 0.0, down(row, t)))
            lower = jnp.where(own_second, 1.0, jnp.where(own_first, 0.0, down(row, t + 1)))
            lead_first = c * upper - b * lower
            lead_second = a * lower - b * upper
            swept = first * lead_first + second * lead_second
            rest = jnp.where(own_first | own_second, 0.0, row) - swept * scale
            row = jnp.where(at_first, lead_first * scale, jnp.where(at_second, lead_second * scale, rest))
            for s in range(t + 2, 8):
                upper, lower = down(cols[s], t), down(cols[s], t + 1)
                lead_first = c * upper - b * lower
                lead_second = a * lower - b * upper
                swept = first * lead_first + second * lead_second
                cols[s] = jnp.where(
                    at_first,
                    lead_first * scale,
                    jnp.where(at_second, lead_second * scale, cols[s] - swept * scale),
                )
        strips[m] = row
        for piece in beside[m * len(beside) // count : (m + 1) * len(beside) // count]:
            piece()
        done = (lanes >= 8 * m) & (lanes < 8 * m + 8)
        leads = [down(row, t) for t in range(8)]
        for b in [*range(m + 1, inside[-1] + 1), *range(inside[0], m)]:
            old = strips[b]
            strips[b] = jnp.where(done, 0.0, old) - total([across(old, 8 * m + t) * leads[t] for t in range(8)])
        if m == inside[-1]:
            reduced = jnp.concatenate(
                [strips[b] if b in inside else jnp.zeros((8, BLK), jnp.float32) for b in range(count)], axis=0
            )
            swept = mm(before, as_right(reduced))
            done = (lanes >= 8 * inside[0]) & (lanes < 8 * inside[-1] + 8)
            for n, b in enumerate(outside):
                strips[b] = jnp.where(done, 0.0, strips[b]) - swept[8 * n : 8 * n + 8, :]
    return jnp.concatenate(strips, axis=0)


def eliminate(src, dst, held, left_ref, right_ref, last=False):
    size = src.shape[0]
    rest = size - BLK
    pivot = held[...]
    scaled = mm(as_left(pivot), as_right(src[0:BLK, BLK:size]))
    left_ref[...] = as_left(src[BLK:size, 0:BLK])
    right_ref[...] = as_right(scaled)
    dst[rest:size, 0:rest] = scaled
    dst[rest:size, rest:size] = pivot

    def strip(top, tall, at, wide):
        def run():
            dst[top : top + tall, at : at + wide] = src[
                BLK + top : BLK + top + tall, BLK + at : BLK + at + wide
            ] - mm(left_ref[top : top + tall, :], right_ref[:, at : at + wide])

        return run

    def border():
        dst[0:rest, rest:size] = -mm(left_ref[...], as_right(pivot))

    wide = 2 * BLK
    tall = rest if last else rest // 2
    work = [
        strip(top, tall, at, min(wide, rest - at)) for at in range(0, rest, wide) for top in range(0, rest, tall)
    ] + [border]
    if last:
        for piece in work:
            piece()
    else:
        ahead = src[BLK : 2 * BLK, BLK : 2 * BLK] - mm(left_ref[0:BLK, :], right_ref[:, 0:BLK])
        held[...] = invert_block(ahead, work)


def gram_kernel(ev_ref, own_ref, other_ref, valid_ref, *refs):
    parts, turned_ref, chip = refs[:-2], refs[-2], refs[-1]
    here = ev_ref[0]
    rows, width = own_ref.shape
    blocks = width // BLK
    half = blocks // 2
    middle = width // 2
    for order, ref in ((here, own_ref), (1 - here, other_ref)):
        at = pl.ds(pl.multiple_of(order * rows, rows), rows)
        for side in range(2):
            to = pl.ds(pl.multiple_of((here + side) % 2 * middle, middle), middle)
            piece = ref[:, side * middle : (side + 1) * middle]
            chip[at, to] = piece
            turned_ref[to, at] = piece.T
    turned_ref[...] = turned_ref[...] * valid_ref[...].astype(jnp.float32).astype(jnp.bfloat16)
    spots = [(ref, at) for ref in parts for at in range(0, ref.shape[0], BLK)]
    for i in range(half):
        part = mm(
            turned_ref[i * BLK : (i + 1) * BLK, :],
            chip[:, i * BLK : (i + half) * BLK],
        )
        for j in range(half):
            ref, at = spots[i * half + j]
            ref[at : at + BLK, :] = part[:, j * BLK : (j + 1) * BLK]
    for t in range(half // 2):
        i = here * (half // 2) + t
        ref, at = spots[half * half + t]
        ref[at : at + BLK, :] = mm(
            turned_ref[pl.ds(pl.multiple_of(i * BLK, BLK), BLK), :],
            chip[:, pl.ds(pl.multiple_of((i + half) * BLK, BLK), BLK)],
        )


def inverse_kernel(total_rows, stages, first, last, *refs):
    if first:
        ev_ref, *parts, matrix_out, held_out, one, two, left_ref, right_ref = refs
    elif last:
        place_ref, matrix_in, held_in, turned_ref, out_ref, one, two, held_out, placed, left_ref, right_ref = refs
    else:
        matrix_in, held_in, matrix_out, held_out, one, two, left_ref, right_ref = refs
    size = one.shape[0]
    blocks = size // BLK
    half = blocks // 2
    if first:
        spots = [(ref, at) for ref in parts for at in range(0, ref.shape[0], BLK)]
        rows = lax.broadcasted_iota(jnp.int32, (BLK, BLK), 0)
        cols = lax.broadcasted_iota(jnp.int32, (BLK, BLK), 1)
        ridge = jnp.where(rows == cols, jnp.float32(damping), 0.0)
        count = len(spots) // 2
        for i in range(blocks):
            for j in range(half):
                ref, at = spots[i // half * count + i % half * half + j]
                c = (i + j) % blocks
                value = ref[at : at + BLK, :] / total_rows
                if j == 0:
                    value = value + ridge
                one[i * BLK : (i + 1) * BLK, c * BLK : (c + 1) * BLK] = value
                if j > 0:
                    one[c * BLK : (c + 1) * BLK, i * BLK : (i + 1) * BLK] = value.T
        for side in range(2):
            for t in range(half // 2):
                ref, at = spots[side * count + half * half + t]
                i = (ev_ref[0] + side) % 2 * (half // 2) + t
                value = ref[at : at + BLK, :] / total_rows
                upper = pl.ds(pl.multiple_of(i * BLK, BLK), BLK)
                lower = pl.ds(pl.multiple_of((i + half) * BLK, BLK), BLK)
                one[upper, lower] = value.T if side else value
                one[lower, upper] = value if side else value.T
        held_out[...] = invert_block(one[0:BLK, 0:BLK])
        now = one
    else:
        held_out[...] = held_in[...]
        now = matrix_in
    for stage in range(stages):
        if stage == stages - 1 and not last:
            then = matrix_out
        else:
            then = one if now is two else two
        eliminate(now, then, held_out, left_ref, right_ref, last=last and stage == stages - 1)
        now = then
    if last:
        for i in range(blocks):
            to = pl.ds(pl.multiple_of(place_ref[i] * BLK, BLK), BLK)
            placed[to, :] = now[i * BLK : (i + 1) * BLK, :].astype(jnp.bfloat16)
        wide = 2 * BLK
        for at in range(0, out_ref.shape[1], wide):
            out_ref[:, at : at + wide] = mm(placed[...], turned_ref[:, at : at + wide]).astype(jnp.bfloat16)


def call_inverse(width, total_rows, stages, operands, first=False, last=False):
    state = (
        jax.ShapeDtypeStruct((width, width), jnp.float32),
        jax.ShapeDtypeStruct((BLK, BLK), jnp.float32),
    )
    result = jax.ShapeDtypeStruct((width, operands[-1].shape[-1]), jnp.bfloat16)
    return pl.pallas_call(
        functools.partial(inverse_kernel, total_rows, stages, first, last),
        out_shape=result if last else state,
        in_specs=[SMEM if x.ndim == 1 else VMEM for x in operands],
        out_specs=VMEM if last else (VMEM, VMEM),
        scratch_shapes=[
            pltpu.VMEM((width, width), jnp.float32),
            pltpu.VMEM((width, width), jnp.float32),
            *([pltpu.VMEM((BLK, BLK), jnp.float32), pltpu.VMEM((width, width), jnp.bfloat16)] if last else []),
            pltpu.VMEM((width - BLK, 6 * BLK), jnp.bfloat16),
            pltpu.VMEM((6 * BLK, width - BLK), jnp.bfloat16),
        ],
        compiler_params=pltpu.CompilerParams(vmem_limit_bytes=36 * MIB),
        cost_estimate=pl.CostEstimate(flops=stages * 6_000_000_000, bytes_accessed=4 * MIB, transcendentals=0),
        name="inverse",
    )(*operands)


def score_kernel(halves, bucket_ref, precond_ref, *refs):
    *eval_refs, out_ref = refs
    width = precond_ref.shape[0]
    bucket = bucket_ref[0]
    weight = jnp.zeros(bucket.shape, jnp.float32)
    for level in range(BUCKETS):
        weight = weight + jnp.where(bucket == level, jnp.float32(weight_table[level]), 0.0)
    weight = weight / jnp.sqrt(jnp.float32(width))
    rows = out_ref.shape[0]
    evals = []
    for count in halves:
        some, eval_refs = eval_refs[:count], eval_refs[count:]
        value = some[0][...]
        if count == 2:
            value = jnp.where(pl.program_id(0) < pl.num_programs(0) // 2, value, some[1][...])
        evals.append(value)
    evals = jnp.concatenate(evals, axis=1)
    scores = mm(evals, precond_ref[...])
    for at in range(0, rows, BLK):
        factor = jnp.broadcast_to(weight[:, at : at + BLK], (BLK, BLK)).T
        for to in range(0, out_ref.shape[1], BLK):
            out_ref[at : at + BLK, to : to + BLK] = (
                scores[at : at + BLK, to : to + BLK] * factor
            ).astype(jnp.bfloat16)


def shift(members, stride, by):
    n = lax.axis_size("tr")
    pairs = []
    for i in range(n):
        p = i // stride % members
        pairs.append((i, i + ((p + by) % members - p) * stride))
    return pairs


def scatter_sum(x, members, stride):
    me = lax.axis_index("tr") // stride % members
    chunks = x.reshape(members, -1, BLK)
    mine = lax.dynamic_index_in_dim(chunks, me, keepdims=False)
    got = [
        lax.ppermute(
            lax.dynamic_index_in_dim(chunks, (me + by) % members, keepdims=False), "tr", shift(members, stride, by)
        )
        for by in range(1, members)
    ]
    for piece in got:
        mine = mine + piece
    return mine


def collect(x, members, stride):
    me = lax.axis_index("tr") // stride % members
    got = [x] + [lax.ppermute(x, "tr", shift(members, stride, by)) for by in range(members - 1, 0, -1)]
    if members == 2:
        whole = jnp.where(
            me == 0, jnp.concatenate(got, axis=0), jnp.concatenate(got[::-1], axis=0)
        )
        return whole
    twice = jnp.concatenate(got + got, axis=0)
    return lax.dynamic_slice_in_dim(twice, (members - me) * x.shape[0], members * x.shape[0])


def chip_axes():
    n = lax.axis_size("tr")
    inner = 2 ** ((n.bit_length() - 1) // 2)
    return (inner, 1), (n // inner, inner)


def sum_over_tr(parts):
    axes = chip_axes()
    orders = [axes, axes[::-1]]
    parts = [scatter_sum(x, *order[0]) for x, order in zip(parts, orders)]
    parts = [scatter_sum(x, *order[1]) for x, order in zip(parts, orders)]
    parts = lax.optimization_barrier([collect(x, *order[1]) for x, order in zip(parts, orders)])
    return [collect(x, *order[0]) for x, order in zip(parts, orders)]


def shards(train_grads, eval_grads, eval_bucket, train_valid):
    rows_here, width = train_grads.shape
    total_rows = rows_here * lax.axis_size("tr") * lax.axis_size("ev")
    here = lax.axis_index("ev")
    tr = lax.axis_index("tr")
    swap = [(0, 1), (1, 0)]
    blocks = width // BLK
    half = blocks // 2
    (inner, _), (outer, _) = chip_axes()
    by_ring = eval_grads.shape[1] % BLK == 0

    def across_inner(x):
        return [lax.ppermute(x, "tr", shift(inner, 1, by)) for by in range(1, inner)]

    def along_outer(x):
        return lax.ppermute(x, "tr", shift(outer, inner, 1))

    other_train = lax.ppermute(train_grads, "ev", swap)
    other_valid = lax.ppermute(train_valid, "ev", swap)
    chip_valid = jnp.where(
        here == 0, jnp.concatenate([train_valid, other_valid]), jnp.concatenate([other_valid, train_valid])
    )
    chip_rows = 2 * rows_here
    held = half * (2 * half + 1) // 2 * BLK
    first_held = held // BLK * 13 // 20 * BLK
    *local_gram, turned = pl.pallas_call(
        gram_kernel,
        out_shape=(
            jax.ShapeDtypeStruct((first_held, BLK), jnp.float32),
            jax.ShapeDtypeStruct((held - first_held, BLK), jnp.float32),
            jax.ShapeDtypeStruct((width, chip_rows), jnp.bfloat16),
        ),
        in_specs=[SMEM, VMEM, VMEM, VMEM],
        out_specs=(VMEM,) * 3,
        scratch_shapes=[pltpu.VMEM((chip_rows, width), jnp.bfloat16)],
        compiler_params=pltpu.CompilerParams(vmem_limit_bytes=32 * MIB),
        cost_estimate=pl.CostEstimate(flops=2 * chip_rows * held * BLK, bytes_accessed=6 * MIB, transcendentals=0),
        name="gram",
    )(here.reshape(1), train_grads, other_train, chip_valid[None, :])

    ring = [eval_grads]
    beside = []
    if by_ring:
        ring.append(along_outer(eval_grads))
        beside.append(across_inner(eval_grads))
        local_gram, ring, beside = lax.optimization_barrier((local_gram, ring, beside))

    own_gram = sum_over_tr(local_gram)
    other_gram = [lax.ppermute(x, "ev", swap) for x in own_gram]
    gram = [*own_gram, *other_gram]

    column = (jnp.arange(blocks, dtype=jnp.int32) + half * here) % blocks
    if by_ring:
        gram, ring, beside = lax.optimization_barrier((gram, ring, beside))
        owner = column * BLK // eval_grads.shape[1]
        behind = (tr // inner - owner // inner) % outer
        aside = (tr - owner) % inner
        each = eval_grads.shape[1] // BLK
        place = (behind * inner + aside) * each + column % each
    else:
        gram, eval_grads = lax.optimization_barrier((gram, eval_grads))
        full_eval = lax.all_gather(eval_grads, "tr", axis=1, tiled=True)
        place = column

    def advance():
        if by_ring and len(ring) < outer:
            arrived = ring[-1]
            ring.append(along_outer(arrived))
            beside.append(across_inner(arrived))

    advance()
    state = call_inverse(width, total_rows, 2, (here.reshape(1), *gram), first=True)
    if by_ring:
        state, ring, beside = lax.optimization_barrier((state, ring, beside))
    advance()
    state = call_inverse(width, total_rows, 3, state)
    if by_ring:
        state, ring, beside = lax.optimization_barrier((state, ring, beside))
        while len(ring) < outer:
            advance()
        evals = []
        for arrived, aside in zip(ring, beside):
            evals.append([arrived])
            evals += [[x] for x in aside]
        rows = ring[-1].shape[0] // 2
        for by, before in enumerate(beside[-1], 1):
            top = lax.ppermute(ring[-1][:rows], "tr", shift(inner, 1, by))
            low = along_outer(before[rows:])
            if by == 1:
                evals.append([ring[-1]])
            evals.append([top, low])
    else:
        evals = [[full_eval]]
    precond = call_inverse(width, total_rows, blocks - 5, (place, *state, turned), last=True)

    eval_rows = sum(x.shape[0] for x in evals[0])
    tile = 512
    tiles = eval_rows // tile
    pieces = [x for block in evals for x in block]
    halves = [len(block) for block in evals]
    specs = []
    for block in evals:
        for n, x in enumerate(block):
            each = tiles // len(block)
            specs.append(
                pl.BlockSpec((tile, x.shape[1]), lambda i, low=n * each, each=each: (jnp.clip(i - low, 0, each - 1), 0))
            )
    return pl.pallas_call(
        functools.partial(score_kernel, halves),
        grid=(eval_rows // tile,),
        out_shape=jax.ShapeDtypeStruct((eval_rows, chip_rows), jnp.bfloat16),
        in_specs=[
            pl.BlockSpec((1, 1, tile), lambda i: (i, 0, 0)),
            pl.BlockSpec((width, chip_rows), lambda i: (0, 0)),
            *specs,
        ],
        out_specs=pl.BlockSpec((tile, chip_rows), lambda i: (i, 0)),
        compiler_params=pltpu.CompilerParams(vmem_limit_bytes=24 * MIB),
        cost_estimate=pl.CostEstimate(
            flops=2 * eval_rows * width * chip_rows, bytes_accessed=10 * MIB, transcendentals=0
        ),
        name="scores",
    )(eval_bucket.reshape(eval_rows // tile, 1, tile), precond, *pieces)


def solution(mesh):
    in_specs = (
        P(("grp", "tr", "ev"), None),
        P(("grp", "ev"), "tr"),
        P(("grp", "ev")),
        P(("grp", "tr", "ev")),
    )
    out_specs = P(("grp", "ev"), "tr")
    return jax.shard_map(shards, mesh=mesh, in_specs=in_specs, out_specs=out_specs, check_vma=False)
```
